32 devices in a mesh: day: 2 (over y), tm: 4 (over z), sta: 4 (over x, core).
Axes of the slice: x: 2, y: 2, z: 4, core: 2. Of those that a mesh axis runs over, the one named last changes fastest.
Arguments:
- traces: bfloat16 [2048, 24576], P('sta', ('day', 'tm')), parts along dimension 1, may hold values from -12 to 12
- offsets: int32 [24], P(('day', 'tm')), parts along dimension 0, may hold values from 0 to 3072, as said below
- pair_first: int32 [2048], P('sta'), may hold values from 0 to 511
- pair_slot: int32 [2048], P('sta'), may hold values from 0 to 127, as said below
- send_rows: int32 [4, 128], P('sta'), may hold values from 0 to 511, as said below
Outputs:
- correlations: float32 [2048, 2048], P(('day', 'tm'), 'sta'), parts along dimension 0
The draws below stay inside these ranges and needn't reach their ends.
There are 2 independent parts, one for each index of `day`. The reference program is written for one: setup_inputs(seed, part) draws one part's arguments, and reference() takes and returns one part's arrays. A program takes and returns all parts, laid end to end along the dimension named above; an argument that names none is the same for every part. Nothing has to cross between parts.
Inputs may be any that keep to these rules, and one draw needn't show every extreme that they name: offsets[t * 3 + w] lies between w * 1024 and (w + 1) * 1024. For a pair owned by group g whose src = pair_slot // 32 lies two or more groups from g around the cycle of 4 groups (neither g - 1, g nor g + 1 modulo 4), pair_slot mod 32 is below 8. The 32 entries send_rows[s, g * 32 .. (g + 1) * 32 - 1] are distinct.
All inputs are finite; a program needn't handle non-finite values.
Results may differ from the reference program's by a relative error of at most 0.0039.
Values may be sent and summed in bfloat16 or wider, within the bound.
A program may use at most 64 MiB of HBM per device.

```python
import math
import jax
import jax.numpy as jnp
from jax import lax

STATIONS = 2048
STA_GROUP = 512
WIN = 2048
NF = 512
STEP = 1024
NWB = 3
TB = 3072
SAMPLES = 12288
WINDOWS = 12
CAP = 32
CAP_FAR = 8
PD = 512
PAIRS = 2048
NL = 1024
N_TM = 4


def draw_traces(key, part):
    noise_key, scale_key = jax.random.split(key, 2)
    station_scale = jnp.exp(jax.random.uniform(scale_key, (STATIONS, 1), jnp.float32, math.log(0.03), math.log(3.0)))
    values = station_scale * jax.random.normal(noise_key, (STATIONS, SAMPLES), jnp.float32)
    return jnp.clip(values, -12.0, 12.0).astype(jnp.bfloat16)


def draw_offsets(key, part):
    jitter_key, low_key, high_key = jax.random.split(key, 3)
    blocks = WINDOWS // NWB
    jitter = jax.random.randint(jitter_key, (blocks, NWB), 0, STEP + 1)
    low_block = jax.random.randint(low_key, (), 0, blocks)
    high_block = jax.random.randint(high_key, (), 0, blocks)
    block_index = jnp.arange(blocks)[:, None]
    window_index = jnp.arange(NWB)[None, :]
    jitter = jnp.where((block_index == low_block) & (window_index == 0), 0, jitter)
    jitter = jnp.where((block_index == high_block) & (window_index == NWB - 1), STEP, jitter)
    return (window_index * STEP + jitter).reshape(WINDOWS).astype(jnp.int32)


def draw_pair_first(key, part):
    groups = PAIRS // PD

    def take_one(subkey):
        shuffled = jax.random.permutation(subkey, STA_GROUP)
        return shuffled[jnp.arange(PD) % STA_GROUP]
    return jax.vmap(take_one)(jax.random.split(key, groups)).reshape(PAIRS).astype(jnp.int32)


def draw_pair_slot(key, part):
    groups = PAIRS // PD
    count_key, full_key, source_key, pick_key = jax.random.split(key, 4)
    owner_index = jnp.arange(groups)[:, None]
    source_index = jnp.arange(groups)[None, :]
    distance = jnp.abs(owner_index - source_index)
    distance = jnp.minimum(distance, groups - distance)
    lowest = jnp.where(distance <= 1, max(CAP // 2, 1), 1)
    highest = jnp.where(distance <= 1, CAP + 1, CAP_FAR + 1)
    counts = jax.random.randint(count_key, (groups, groups), lowest, highest)
    counts = jnp.where(distance == 0, CAP, counts)
    full_owner = jax.random.randint(full_key, (), 0, groups)
    counts = jnp.where((owner_index == full_owner) & (distance <= 1), CAP, counts)
    far_source = (full_owner + 2) % groups
    counts = jnp.where((owner_index == full_owner) & (source_index == far_source), CAP_FAR, counts)
    pair_index = jnp.arange(PD)[None, :]
    pick_source = jnp.where(pair_index < groups * CAP, pair_index // CAP, jax.random.randint(source_key, (groups, PD), 0, groups))
    live_count = jnp.take_along_axis(counts, pick_source, axis=1)
    random_slot = jax.random.randint(pick_key, (groups, PD), 0, live_count)
    direct = pair_index % CAP
    slot_inside = jnp.where((pair_index < groups * CAP) & (direct < live_count), direct, random_slot)
    return (pick_source * CAP + slot_inside).reshape(PAIRS).astype(jnp.int32)


def draw_send_rows(key, part):
    groups = STATIONS // STA_GROUP
    blocks = groups * groups
    subkeys = jax.random.split(key, blocks + 1)

    def take_one(subkey):
        return jax.random.permutation(subkey, STA_GROUP)[:CAP]
    regular = jax.vmap(take_one)(subkeys[:blocks]).astype(jnp.int32)
    inner_rows = 1 + jax.random.permutation(subkeys[blocks], STA_GROUP - 2)[:CAP - 2]
    special = jnp.concatenate([jnp.array([0, STA_GROUP - 1], jnp.int32), inner_rows.astype(jnp.int32)])
    chosen = jax.random.randint(jax.random.fold_in(key, 7), (), 0, blocks)
    rows_all = jnp.where((jnp.arange(blocks) == chosen)[:, None], special[None, :], regular)
    return rows_all.reshape(groups, groups * CAP).astype(jnp.int32)


def setup_inputs(seed: int = 0, part: int = 0) -> dict:
    seeds = jax.random.split(jax.random.key(seed), 6)
    own_keys = jax.random.split(jax.random.fold_in(seeds[5], part), 6)
    traces = draw_traces(jax.random.fold_in(jax.random.fold_in(seeds[5], part), 71), part)
    offsets = draw_offsets(jax.random.fold_in(jax.random.fold_in(seeds[5], part), 71), part)
    pair_first = draw_pair_first(jax.random.fold_in(seeds[5], 71), part)
    pair_slot = draw_pair_slot(jax.random.fold_in(seeds[5], 71), part)
    send_rows = draw_send_rows(jax.random.fold_in(seeds[5], 71), part)
    return dict(traces=traces, offsets=offsets, pair_first=pair_first, pair_slot=pair_slot, send_rows=send_rows)


FLOOR = 0.1

def taper_table(length):
    sample_index = jnp.arange(length, dtype=jnp.float32)
    return 0.5 - 0.5 * jnp.cos(2.0 * math.pi * sample_index / length)

def dft_table(length, bin_count):
    sample_index = jnp.arange(length, dtype=jnp.int32)[:, None]
    bin_index = jnp.arange(bin_count, dtype=jnp.int32)[None, :] + 1
    angles = (sample_index * bin_index % length).astype(jnp.float32) * (2.0 * math.pi / length)
    return jnp.concatenate([jnp.cos(angles), -jnp.sin(angles)], axis=1).astype(jnp.bfloat16)

def lag_table(lag_count, length, bin_count):
    lag_shift = jnp.arange(lag_count, dtype=jnp.int32)[:, None] - lag_count // 2
    bin_index = jnp.arange(bin_count, dtype=jnp.int32)[None, :] + 1
    angles = (lag_shift * bin_index % length).astype(jnp.float32) * (2.0 * math.pi / length)
    return jnp.concatenate([jnp.cos(angles), -jnp.sin(angles)], axis=1)

def segments(block_data, starts, length):

    def take_one(start_at):
        return lax.dynamic_slice_in_dim(block_data, start_at, length, axis=1)
    pieces = jax.vmap(take_one)(starts)
    values = pieces.astype(jnp.float32)
    centred = values - lax.optimization_barrier(jnp.mean(values, axis=2, keepdims=True))
    return (centred * taper_table(length)).astype(jnp.bfloat16)

def whiten(spectrum, bin_count):
    real_part = spectrum[..., :bin_count]
    imag_part = spectrum[..., bin_count:]
    amplitude = jnp.sqrt(real_part * real_part + imag_part * imag_part + 1e-06)
    padded = jnp.pad(amplitude, [(0, 0)] * (amplitude.ndim - 1) + [(2, 2)])
    smooth = (padded[..., 0:bin_count] + padded[..., 1:bin_count + 1] + padded[..., 2:bin_count + 2] + padded[..., 3:bin_count + 3] + padded[..., 4:bin_count + 4]) / 5.0
    inverse = 1.0 / jnp.maximum(smooth, FLOOR)
    return (spectrum * jnp.concatenate([inverse, inverse], axis=-1)).astype(jnp.bfloat16)

def cross_terms(first_spec, second_spec, bin_count):
    first_real = first_spec[..., :bin_count].astype(jnp.float32)
    first_imag = first_spec[..., bin_count:].astype(jnp.float32)
    second_real = second_spec[..., :bin_count].astype(jnp.float32)
    second_imag = second_spec[..., bin_count:].astype(jnp.float32)
    return jnp.concatenate([first_real * second_real + first_imag * second_imag, first_imag * second_real - first_real * second_imag], axis=-1)

def reference(traces, offsets, pair_first, pair_slot, send_rows):
    table = dft_table(WIN, NF)
    padded = jnp.concatenate([traces, jnp.zeros((STATIONS, WIN), jnp.bfloat16)], axis=1)
    owner_group = jnp.arange(PAIRS, dtype=jnp.int32) // PD
    first_station = owner_group * STA_GROUP + pair_first
    source = pair_slot // CAP
    column = owner_group * CAP + pair_slot % CAP
    second_station = source * STA_GROUP + send_rows[source, column]

    def block_step(running, block_number):
        block_data = lax.dynamic_slice_in_dim(padded, block_number * TB, TB + WIN, axis=1)
        starts = lax.dynamic_slice_in_dim(offsets, block_number * NWB, NWB)
        segment = segments(block_data, starts, WIN)
        spectrum = jnp.dot(segment.reshape(NWB * STATIONS, WIN), table, preferred_element_type=jnp.float32) * (1.0 / math.sqrt(WIN))
        whitened = whiten(spectrum.reshape(NWB, STATIONS, 2 * NF), NF)
        terms = cross_terms(whitened[:, first_station, :], whitened[:, second_station, :], NF)
        return (running + lax.optimization_barrier(jnp.sum(terms, axis=0)), None)
    cross_sum, _ = lax.scan(block_step, jnp.zeros((PAIRS, 2 * NF), jnp.float32), jnp.arange(N_TM, dtype=jnp.int32))
    lag_rows = lag_table(NL, WIN, NF)
    stacked = jnp.dot(lag_rows, cross_sum.T, precision=lax.Precision.HIGHEST, preferred_element_type=jnp.float32)
    return stacked * (1.0 / math.sqrt(NF * WINDOWS))
```

```python
import functools
import math

import jax
import jax.numpy as jnp
import numpy as np
from jax import lax
from jax.experimental import pallas as pl
from jax.experimental.pallas import tpu as pltpu
from jax.sharding import PartitionSpec as P

WIN = 2048
NF = 512
NL = 1024
STEP = 1024
TB = 3072
CAP = 32
FAR_ROWS = 16
FLOOR = 0.1
CHUNKS = 4
PIECES = 2
BLK = 128
ROWS = 16
MESH = pl.DeviceIdType.MESH


def taper_table():
    n = np.arange(WIN, dtype=np.float64)
    return (0.5 - 0.5 * np.cos(2.0 * np.pi * n / WIN)).astype(np.float32)[None, :]


def dft_table():
    n = np.arange(WIN)[:, None]
    k = np.arange(NF)[None, :] + 1
    angle = (n * k % WIN) * (2.0 * np.pi / WIN)
    return np.concatenate([np.cos(angle), -np.sin(angle)], axis=1).astype(jnp.bfloat16)


def lag_table():
    t = np.arange(NL)[:, None] - NL // 2
    k = np.arange(NF)[None, :] + 1
    angle = (t * k % WIN) * (2.0 * np.pi / WIN)
    return np.concatenate([np.cos(angle), -np.sin(angle)], axis=1).astype(jnp.bfloat16)


def shifted(blocks, jitter):
    quotient = jitter // BLK
    rest = jitter % BLK
    for bit, count in ((8, 24), (4, 20), (2, 18), (1, 17)):
        on = (quotient // bit) % 2 == 1
        blocks = [
            jnp.where(on, blocks[i + bit], blocks[i]) if i + bit < len(blocks) else blocks[i]
            for i in range(count)
        ]
    turn = (BLK - rest) % BLK
    rolled = [pltpu.roll(b, turn, 1) for b in blocks]
    lane = lax.broadcasted_iota(jnp.int32, blocks[0].shape, 1)
    keep = lane < BLK - rest
    return [jnp.where(keep, rolled[i], rolled[i + 1]) for i in range(WIN // BLK)]


def write_segment(blocks, jitter, taper, seg, row):
    values = shifted(blocks, jitter)
    total = values[0]
    for v in values[1:]:
        total = total + v
    mean = jnp.sum(total, axis=1, keepdims=True) * (1.0 / WIN)
    for i, v in enumerate(values):
        columns = slice(i * BLK, (i + 1) * BLK)
        seg[pl.ds(row, ROWS), columns] = ((v - mean) * taper[:, columns]).astype(jnp.bfloat16)


def load_blocks(ref, row, first, count):
    return [
        ref[pl.ds(row, ROWS), i * BLK : (i + 1) * BLK].astype(jnp.float32)
        for i in range(first, first + count)
    ]


def whiten_rows(spec, row):
    re = spec[pl.ds(row, ROWS), :NF]
    im = spec[pl.ds(row, ROWS), NF:]
    amplitude = jnp.sqrt(re * re + im * im + 1e-06)
    wide = jnp.concatenate([amplitude, jnp.zeros((ROWS, BLK), jnp.float32)], axis=1)
    width = NF + BLK
    pair = wide + pltpu.roll(wide, 1, 1)
    five = wide + pltpu.roll(pair, 1, 1) + pltpu.roll(pair, width - 2, 1)
    inverse = 1.0 / jnp.maximum(five[:, :NF] * (1.0 / 5.0), FLOOR)
    return (re * inverse).astype(jnp.bfloat16), (im * inverse).astype(jnp.bfloat16)


def kernel(
    n_tm, n_sta,
    offsets, pair_first, pair_slot, send_rows, taper, traces, table_hbm, lag_hbm,
    out,
    own, rim_prev, rim_next, table, lags, seg, spec, white, outgoing, incoming,
    pick_first, pick_second, pick_send, first_rows, cross_sum, cross,
    up_send, up_recv, down_send, down_recv, offset_send, offset_recv,
    local_sem, rim_send_sem, rim_recv_sem, offset_sem, swap_send_sem, swap_recv_sem,
    up_send_sem, up_recv_sem, down_send_sem, down_recv_sem,
):
    stations = own.shape[0]
    pairs = out.shape[1]
    lag_rows = out.shape[0]
    slots = n_sta * CAP
    chunk = stations // CHUNKS
    tm = lax.axis_index("tm")
    me = lax.axis_index("sta")
    has_prev = tm > 0
    has_next = tm < n_tm - 1
    is_last = tm == n_tm - 1

    copies = [
        pltpu.make_async_copy(traces, own, local_sem.at[0]),
        pltpu.make_async_copy(table_hbm, table, local_sem.at[1]),
        pltpu.make_async_copy(lag_hbm, lags, local_sem.at[2]),
    ]
    for copy in copies:
        copy.start()

    incoming[...] = jnp.zeros_like(incoming)
    offset_send[...] = jnp.full(offset_send.shape, offsets[2], jnp.int32)

    @pl.when(tm == 0)
    def _():
        rim_prev[...] = jnp.zeros_like(rim_prev)
        offset_recv[...] = jnp.full(offset_recv.shape, 2 * STEP, jnp.int32)

    @pl.when(is_last)
    def _():
        rim_next[...] = jnp.zeros_like(rim_next)

    barrier = pltpu.get_barrier_semaphore()
    for delta in range(1, n_sta):
        pl.semaphore_signal(
            barrier, inc=1, device_id={"sta": (me + delta) % n_sta}, device_id_type=MESH
        )

    @pl.when(has_prev)
    def _():
        pl.semaphore_signal(barrier, inc=1, device_id={"tm": tm - 1}, device_id_type=MESH)

    @pl.when(has_next)
    def _():
        pl.semaphore_signal(barrier, inc=1, device_id={"tm": tm + 1}, device_id_type=MESH)

    greeted = n_sta - 1 + has_prev.astype(jnp.int32) + has_next.astype(jnp.int32)
    pl.semaphore_wait(barrier, greeted)

    def rim_up(c):
        rows = pl.ds(c * chunk, chunk)
        return pltpu.make_async_remote_copy(
            src_ref=traces.at[rows, pl.ds(TB - STEP, STEP)],
            dst_ref=rim_prev.at[rows],
            send_sem=rim_send_sem.at[0, c],
            recv_sem=rim_recv_sem.at[0, c],
            device_id={"tm": tm + 1},
            device_id_type=MESH,
        )

    def rim_down(c):
        rows = pl.ds(c * chunk, chunk)
        return pltpu.make_async_remote_copy(
            src_ref=traces.at[rows, pl.ds(0, STEP)],
            dst_ref=rim_next.at[rows],
            send_sem=rim_send_sem.at[1, c],
            recv_sem=rim_recv_sem.at[1, c],
            device_id={"tm": tm - 1},
            device_id_type=MESH,
        )

    offset_up = pltpu.make_async_remote_copy(
        src_ref=offset_send,
        dst_ref=offset_recv,
        send_sem=offset_sem.at[0],
        recv_sem=offset_sem.at[1],
        device_id={"tm": tm + 1},
        device_id_type=MESH,
    )

    @pl.when(has_next)
    def _():
        offset_up.start()

    for c in range(CHUNKS):

        @pl.when(has_next)
        def _():
            rim_up(c).start()

        @pl.when(has_prev)
        def _():
            rim_down(c).start()

    def one_hot(values, count, depth):
        spread = jnp.transpose(
            jnp.broadcast_to(values.astype(jnp.float32), (BLK, count))
        )
        lane = lax.broadcasted_iota(jnp.int32, (count, BLK), 1).astype(jnp.float32)
        return [
            (spread == lane + float(b * BLK)).astype(jnp.float32).astype(jnp.bfloat16)
            for b in range(depth // BLK)
        ]

    for ref, values, count, depth in (
        (pick_first, pair_first, pairs, stations),
        (pick_second, pair_slot, pairs, slots),
        (pick_send, send_rows, slots, stations),
    ):
        for b, block in enumerate(one_hot(values[...], count, depth)):
            ref[:, b * BLK : (b + 1) * BLK] = block

    for copy in copies[:2]:
        copy.wait()

    batch = 2 * chunk

    def transform():
        spec[...] = jnp.dot(
            seg[...], table[...], preferred_element_type=jnp.float32
        ) * (1.0 / math.sqrt(WIN))

    def single_window(slot, jitter, blocks_at):
        @pl.loop(0, stations // batch)
        def _(step):
            start = step * batch

            @pl.loop(0, batch // ROWS)
            def _(g):
                row = pl.multiple_of(start + g * ROWS, ROWS)
                write_segment(
                    blocks_at(row), jitter, taper, seg, pl.multiple_of(g * ROWS, ROWS)
                )

            transform()

            @pl.loop(0, batch // ROWS)
            def _(g):
                re, im = whiten_rows(spec, pl.multiple_of(g * ROWS, ROWS))
                row = pl.multiple_of(start + g * ROWS, ROWS)
                white[slot, pl.ds(row, ROWS), :NF] = re
                white[slot, pl.ds(row, ROWS), NF:] = im

    def swap(which, slot, depth):
        result = []
        for delta in range(1, n_sta):
            rows = CAP if min(delta, n_sta - delta) <= 1 else FAR_ROWS
            partner = (me + delta) % n_sta
            result.append(
                pltpu.make_async_remote_copy(
                    src_ref=outgoing.at[
                        pl.ds(slot, depth), pl.ds(pl.multiple_of(partner * CAP, CAP), rows)
                    ],
                    dst_ref=incoming.at[
                        pl.ds(slot, depth), pl.ds(pl.multiple_of(me * CAP, CAP), rows)
                    ],
                    send_sem=swap_send_sem.at[which, delta],
                    recv_sem=swap_recv_sem.at[which, delta],
                    device_id={"sta": partner},
                    device_id_type=MESH,
                )
            )
        return result

    def start_swap(which, slot, depth):
        for w in range(slot, slot + depth):
            outgoing[w] = jnp.dot(
                pick_send[...], white[w], preferred_element_type=jnp.float32
            ).astype(jnp.bfloat16)
        for copy in swap(which, slot, depth):
            copy.start()
        mine = pl.ds(pl.multiple_of(me * CAP, CAP), CAP)
        for w in range(slot, slot + depth):
            incoming[w, mine] = outgoing[w, mine]

    def end_swap(which, slot, depth):
        for copy in swap(which, slot, depth):
            copy.wait()

    def gather_first(w):
        first_rows[w] = jnp.dot(
            pick_first[...], white[w], preferred_element_type=jnp.float32
        ).astype(jnp.bfloat16)

    part = min(pairs, 256)
    width = 256

    def add_cross(windows, fresh, final):
        @pl.loop(0, pairs // part)
        def _(p):
            rows = pl.ds(pl.multiple_of(p * part, part), part)
            for b in range(NF // width):
                rcol = slice(b * width, (b + 1) * width)
                icol = slice(NF + b * width, NF + (b + 1) * width)
                real = None if fresh else cross_sum[rows, rcol]
                imag = None if fresh else cross_sum[rows, icol]
                for w in windows:
                    fr = first_rows[w, rows, rcol].astype(jnp.float32)
                    fi = first_rows[w, rows, icol].astype(jnp.float32)
                    sr = jnp.dot(
                        pick_second[rows], incoming[w, :, rcol],
                        preferred_element_type=jnp.float32,
                    )
                    si = jnp.dot(
                        pick_second[rows], incoming[w, :, icol],
                        preferred_element_type=jnp.float32,
                    )
                    new_real = fr * sr + fi * si
                    new_imag = fi * sr - fr * si
                    real = new_real if real is None else real + new_real
                    imag = new_imag if imag is None else imag + new_imag
                if final:
                    cross[rows, rcol] = real.astype(jnp.bfloat16)
                    cross[rows, icol] = imag.astype(jnp.bfloat16)
                else:
                    cross_sum[rows, rcol] = real
                    cross_sum[rows, icol] = imag

    single_window(0, offsets[0], lambda row: load_blocks(own, row, 0, 24))
    start_swap(0, 0, 1)

    @pl.when(is_last)
    def _():
        single_window(
            3,
            offsets[2] - 2 * STEP,
            lambda row: load_blocks(own, row, 16, 8)
            + [jnp.zeros((ROWS, BLK), jnp.float32)] * 16,
        )
        start_swap(2, 3, 1)

    gather_first(0)
    end_swap(0, 0, 1)
    add_cross((0,), True, False)

    @pl.when(is_last)
    def _():
        gather_first(3)
        end_swap(2, 3, 1)
        add_cross((3,), False, False)

    @pl.when(has_prev)
    def _():
        offset_up.wait_recv()

    jitter_1 = offsets[1] - STEP
    jitter_2 = offset_recv[0, 0] - 2 * STEP
    keep = jnp.where(has_prev, 1.0, 0.0).astype(jnp.float32)

    @pl.loop(0, CHUNKS)
    def _(c):
        @pl.when(has_prev)
        def _():
            rim_up(c).wait_recv()

        @pl.when(has_next)
        def _():
            rim_down(c).wait_recv()

        start = c * chunk

        @pl.loop(0, chunk // ROWS)
        def _(g):
            row = pl.multiple_of(start + g * ROWS, ROWS)
            at = pl.multiple_of(g * ROWS, ROWS)
            write_segment(
                load_blocks(own, row, 8, 16) + load_blocks(rim_next, row, 0, 8),
                jitter_1, taper, seg, at,
            )
            write_segment(
                load_blocks(rim_prev, row, 0, 8) + load_blocks(own, row, 0, 16),
                jitter_2, taper, seg, pl.multiple_of(chunk + g * ROWS, ROWS),
            )

        transform()

        @pl.loop(0, chunk // ROWS)
        def _(g):
            row = pl.multiple_of(start + g * ROWS, ROWS)
            re, im = whiten_rows(spec, pl.multiple_of(g * ROWS, ROWS))
            white[1, pl.ds(row, ROWS), :NF] = re
            white[1, pl.ds(row, ROWS), NF:] = im
            re, im = whiten_rows(spec, pl.multiple_of(chunk + g * ROWS, ROWS))
            white[2, pl.ds(row, ROWS), :NF] = (re * keep).astype(jnp.bfloat16)
            white[2, pl.ds(row, ROWS), NF:] = (im * keep).astype(jnp.bfloat16)

    start_swap(1, 1, 2)
    gather_first(1)
    gather_first(2)
    copies[2].wait()
    end_swap(1, 1, 2)
    add_cross((1, 2), False, True)

    span = pairs // PIECES

    def share(c, piece):
        return lax.dot_general(
            lags[pl.ds(pl.multiple_of(c * lag_rows, lag_rows), lag_rows)],
            cross[pl.ds(pl.multiple_of(piece * span, span), span)],
            (((1,), (1,)), ((), ())),
            preferred_element_type=jnp.float32,
        )

    def up(index):
        return pltpu.make_async_remote_copy(
            src_ref=up_send.at[index],
            dst_ref=up_recv.at[index],
            send_sem=up_send_sem.at[index],
            recv_sem=up_recv_sem.at[index],
            device_id={"tm": tm + 1},
            device_id_type=MESH,
        )

    def down(index):
        return pltpu.make_async_remote_copy(
            src_ref=down_send.at[index],
            dst_ref=down_recv.at[index],
            send_sem=down_send_sem.at[index],
            recv_sem=down_recv_sem.at[index],
            device_id={"tm": tm - 1},
            device_id_type=MESH,
        )

    @pl.loop(0, (n_tm - 1) * PIECES)
    def _(t):
        up_item = t - tm
        up_chunk = n_tm - 1 - up_item // PIECES
        up_piece = up_item % PIECES

        @pl.when((up_item >= 0) & (up_item < (n_tm - 1 - tm) * PIECES))
        def _():
            index = up_chunk * PIECES + up_piece
            own_share = share(up_chunk, up_piece)

            @pl.when(has_prev)
            def _():
                up(index).wait_recv()
                up_send[index] = (own_share + up_recv[index].astype(jnp.float32)).astype(
                    jnp.bfloat16
                )

            @pl.when(tm == 0)
            def _():
                up_send[index] = own_share.astype(jnp.bfloat16)

            up(index).start()

        down_item = t - (n_tm - 1 - tm)
        down_chunk = down_item // PIECES
        down_piece = down_item % PIECES

        @pl.when((down_item >= 0) & (down_item < tm * PIECES))
        def _():
            index = down_chunk * PIECES + down_piece
            own_share = share(down_chunk, down_piece)

            @pl.when(has_next)
            def _():
                down(index).wait_recv()
                down_send[index] = (own_share + down_recv[index].astype(jnp.float32)).astype(
                    jnp.bfloat16
                )

            @pl.when(is_last)
            def _():
                down_send[index] = own_share.astype(jnp.bfloat16)

            down(index).start()

    scaling = 1.0 / math.sqrt(NF * 3 * n_tm)
    for piece in range(PIECES):
        index = tm * PIECES + piece
        columns = slice(piece * span, (piece + 1) * span)
        out[:, columns] = share(tm, piece) * scaling

    for piece in range(PIECES):
        index = tm * PIECES + piece
        columns = slice(piece * span, (piece + 1) * span)

        @pl.when(has_prev)
        def _():
            up(index).wait_recv()
            out[:, columns] += up_recv[index].astype(jnp.float32) * scaling

        @pl.when(has_next)
        def _():
            down(index).wait_recv()
            out[:, columns] += down_recv[index].astype(jnp.float32) * scaling

    @pl.when(has_next)
    def _():
        offset_up.wait_send()

    for c in range(CHUNKS):

        @pl.when(has_next)
        def _():
            rim_up(c).wait_send()

        @pl.when(has_prev)
        def _():
            rim_down(c).wait_send()

    @pl.loop(0, n_tm * PIECES)
    def _(index):
        @pl.when(index >= (tm + 1) * PIECES)
        def _():
            up(index).wait_send()

        @pl.when(index < tm * PIECES)
        def _():
            down(index).wait_send()


def on_device(n_tm, n_sta, traces, offsets, pair_first, pair_slot, send_rows):
    stations = traces.shape[0]
    pairs = pair_first.shape[0]
    slots = n_sta * CAP
    lag_rows = NL // n_tm
    chunk = stations // CHUNKS
    items = n_tm * PIECES
    bf16, f32 = jnp.bfloat16, jnp.float32
    vmem = pl.BlockSpec(memory_space=pltpu.VMEM)
    smem = pl.BlockSpec(memory_space=pltpu.SMEM)
    hbm = pl.BlockSpec(memory_space=pl.ANY)
    dma = pltpu.SemaphoreType.DMA
    strip = pltpu.VMEM((items, lag_rows, pairs // PIECES), bf16)
    return pl.pallas_call(
        functools.partial(kernel, n_tm, n_sta),
        out_shape=jax.ShapeDtypeStruct((lag_rows, pairs), f32),
        in_specs=[smem, vmem, vmem, vmem, vmem, hbm, hbm, hbm],
        out_specs=vmem,
        scratch_shapes=[
            pltpu.VMEM((stations, TB), bf16),
            pltpu.VMEM((stations, STEP), bf16),
            pltpu.VMEM((stations, STEP), bf16),
            pltpu.VMEM((WIN, 2 * NF), bf16),
            pltpu.VMEM((NL, 2 * NF), bf16),
            pltpu.VMEM((2 * chunk, WIN), bf16),
            pltpu.VMEM((2 * chunk, 2 * NF), f32),
            pltpu.VMEM((4, stations, 2 * NF), bf16),
            pltpu.VMEM((4, slots, 2 * NF), bf16),
            pltpu.VMEM((4, slots, 2 * NF), bf16),
            pltpu.VMEM((pairs, stations), bf16),
            pltpu.VMEM((pairs, slots), bf16),
            pltpu.VMEM((slots, stations), bf16),
            pltpu.VMEM((4, pairs, 2 * NF), bf16),
            pltpu.VMEM((pairs, 2 * NF), f32),
            pltpu.VMEM((pairs, 2 * NF), bf16),
            strip,
            strip,
            strip,
            strip,
            pltpu.VMEM((8, BLK), jnp.int32),
            pltpu.VMEM((8, BLK), jnp.int32),
            dma((3,)),
            dma((2, CHUNKS)),
            dma((2, CHUNKS)),
            dma((2,)),
            dma((3, n_sta)),
            dma((3, n_sta)),
            dma((items,)),
            dma((items,)),
            dma((items,)),
            dma((items,)),
        ],
        compiler_params=pltpu.CompilerParams(
            collective_id=0, has_side_effects=True, vmem_limit_bytes=56 * 1024 * 1024
        ),
    )(
        offsets,
        pair_first.reshape(1, pairs),
        pair_slot.reshape(1, pairs),
        send_rows,
        jnp.asarray(taper_table()),
        traces,
        jnp.asarray(dft_table()),
        jnp.asarray(lag_table()),
    )


def solution(mesh):
    in_specs = (P("sta", ("day", "tm")), P(("day", "tm")), P("sta"), P("sta"), P("sta", None))
    out_specs = P(("day", "tm"), "sta")
    return jax.shard_map(
        functools.partial(on_device, mesh.shape["tm"], mesh.shape["sta"]),
        mesh=mesh,
        in_specs=in_specs,
        out_specs=out_specs,
        check_vma=False,
    )
```

```python
import functools
import math

import jax
import jax.numpy as jnp
import numpy as np
from jax import lax
from jax.experimental import pallas as pl
from jax.experimental.pallas import tpu as pltpu
from jax.sharding import PartitionSpec as P

WIN = 2048
NF = 512
NL = 1024
STEP = 1024
TB = 3072
CAP = 32
FAR_ROWS = 16
FLOOR = 0.1
CHUNKS = 4
PIECES = 2
BLK = 128
ROWS = 16
MESH = pl.DeviceIdType.MESH


def taper_table():
    n = np.arange(WIN, dtype=np.float64)
    return (0.5 - 0.5 * np.cos(2.0 * np.pi * n / WIN)).astype(np.float32)[None, :]


def dft_table():
    n = np.arange(WIN)[:, None]
    k = np.arange(NF)[None, :] + 1
    angle = (n * k % WIN) * (2.0 * np.pi / WIN)
    return np.concatenate([np.cos(angle), -np.sin(angle)], axis=1).astype(jnp.bfloat16)


def lag_table():
    t = np.arange(NL)[:, None] - NL // 2
    k = np.arange(NF)[None, :] + 1
    angle = (t * k % WIN) * (2.0 * np.pi / WIN)
    return np.concatenate([np.cos(angle), -np.sin(angle)], axis=1).astype(jnp.bfloat16)


def shifted(blocks, jitter):
    quotient = jitter // BLK
    rest = jitter % BLK
    for bit, count in ((8, 24), (4, 20), (2, 18), (1, 17)):
        on = (quotient // bit) % 2 == 1
        blocks = [
            jnp.where(on, blocks[i + bit], blocks[i]) if i + bit < len(blocks) else blocks[i]
            for i in range(count)
        ]
    turn = (BLK - rest) % BLK
    rolled = [pltpu.roll(b, turn, 1) for b in blocks]
    lane = lax.broadcasted_iota(jnp.int32, blocks[0].shape, 1)
    keep = lane < BLK - rest
    return [jnp.where(keep, rolled[i], rolled[i + 1]) for i in range(WIN // BLK)]


def write_segment(blocks, jitter, taper, seg, row):
    values = shifted(blocks, jitter)
    sums = values
    while len(sums) > 1:
        sums = [a + b for a, b in zip(sums[::2], sums[1::2])]
    total = sums[0]
    mean = jnp.sum(total, axis=1, keepdims=True) * (1.0 / WIN)
    for i, v in enumerate(values):
        columns = slice(i * BLK, (i + 1) * BLK)
        seg[pl.ds(row, ROWS), columns] = ((v - mean) * taper[:, columns]).astype(jnp.bfloat16)


def load_blocks(ref, row, first, count):
    return [
        ref[pl.ds(row, ROWS), i * BLK : (i + 1) * BLK].astype(jnp.float32)
        for i in range(first, first + count)
    ]


def whiten_rows(spec, row):
    re = spec[pl.ds(row, ROWS), :NF]
    im = spec[pl.ds(row, ROWS), NF:]
    amplitude = jnp.sqrt(re * re + im * im + 1e-06)
    wide = jnp.concatenate([amplitude, jnp.zeros((ROWS, BLK), jnp.float32)], axis=1)
    width = NF + BLK
    pair = wide + pltpu.roll(wide, 1, 1)
    five = wide + pltpu.roll(pair, 1, 1) + pltpu.roll(pair, width - 2, 1)
    inverse = 1.0 / jnp.maximum(five[:, :NF] * (1.0 / 5.0), FLOOR)
    return (re * inverse).astype(jnp.bfloat16), (im * inverse).astype(jnp.bfloat16)


def kernel(
    n_tm, n_sta,
    offsets, pair_first, pair_slot, send_rows, taper, traces, table_hbm, lag_hbm,
    out,
    own, rim_prev, rim_next, table, lags, seg, spec, white, outgoing, incoming,
    pick_first, pick_second, pick_send, first_rows, cross_sum, cross,
    up_send, up_recv, down_send, down_recv, offset_send, offset_recv,
    local_sem, rim_send_sem, rim_recv_sem, offset_sem, swap_send_sem, swap_recv_sem,
    up_send_sem, up_recv_sem, down_send_sem, down_recv_sem,
):
    stations = own.shape[0]
    pairs = out.shape[1]
    lag_rows = out.shape[0]
    slots = n_sta * CAP
    chunk = stations // CHUNKS
    tm = lax.axis_index("tm")
    me = lax.axis_index("sta")
    has_prev = tm > 0
    has_next = tm < n_tm - 1
    is_last = tm == n_tm - 1

    copies = [
        pltpu.make_async_copy(traces, own, local_sem.at[0]),
        pltpu.make_async_copy(table_hbm, table, local_sem.at[1]),
        pltpu.make_async_copy(lag_hbm, lags, local_sem.at[2]),
    ]
    for copy in copies:
        copy.start()

    incoming[...] = jnp.zeros_like(incoming)
    offset_send[...] = jnp.full(offset_send.shape, offsets[2], jnp.int32)

    @pl.when(tm == 0)
    def _():
        rim_prev[...] = jnp.zeros_like(rim_prev)
        offset_recv[...] = jnp.full(offset_recv.shape, 2 * STEP, jnp.int32)

    @pl.when(is_last)
    def _():
        rim_next[...] = jnp.zeros_like(rim_next)

    barrier = pltpu.get_barrier_semaphore()
    for delta in range(1, n_sta):
        pl.semaphore_signal(
            barrier, inc=1, device_id={"sta": (me + delta) % n_sta}, device_id_type=MESH
        )

    @pl.when(has_prev)
    def _():
        pl.semaphore_signal(barrier, inc=1, device_id={"tm": tm - 1}, device_id_type=MESH)

    @pl.when(has_next)
    def _():
        pl.semaphore_signal(barrier, inc=1, device_id={"tm": tm + 1}, device_id_type=MESH)

    greeted = n_sta - 1 + has_prev.astype(jnp.int32) + has_next.astype(jnp.int32)
    pl.semaphore_wait(barrier, greeted)

    def rim_up(c):
        rows = pl.ds(c * chunk, chunk)
        return pltpu.make_async_remote_copy(
            src_ref=traces.at[rows, pl.ds(TB - STEP, STEP)],
            dst_ref=rim_prev.at[rows],
            send_sem=rim_send_sem.at[0, c],
            recv_sem=rim_recv_sem.at[0, c],
            device_id={"tm": tm + 1},
            device_id_type=MESH,
        )

    def rim_down(c):
        rows = pl.ds(c * chunk, chunk)
        return pltpu.make_async_remote_copy(
            src_ref=traces.at[rows, pl.ds(0, STEP)],
            dst_ref=rim_next.at[rows],
            send_sem=rim_send_sem.at[1, c],
            recv_sem=rim_recv_sem.at[1, c],
            device_id={"tm": tm - 1},
            device_id_type=MESH,
        )

    offset_up = pltpu.make_async_remote_copy(
        src_ref=offset_send,
        dst_ref=offset_recv,
        send_sem=offset_sem.at[0],
        recv_sem=offset_sem.at[1],
        device_id={"tm": tm + 1},
        device_id_type=MESH,
    )

    @pl.when(has_next)
    def _():
        offset_up.start()

    for c in range(CHUNKS):

        @pl.when(has_next)
        def _():
            rim_up(c).start()

        @pl.when(has_prev)
        def _():
            rim_down(c).start()

    def one_hot(values, count, depth):
        spread = jnp.transpose(
            jnp.broadcast_to(values.astype(jnp.float32), (BLK, count))
        )
        lane = lax.broadcasted_iota(jnp.int32, (count, BLK), 1).astype(jnp.float32)
        return [
            (spread == lane + float(b * BLK)).astype(jnp.float32).astype(jnp.bfloat16)
            for b in range(depth // BLK)
        ]

    for ref, values, count, depth in (
        (pick_first, pair_first, pairs, stations),
        (pick_second, pair_slot, pairs, slots),
        (pick_send, send_rows, slots, stations),
    ):
        for b, block in enumerate(one_hot(values[...], count, depth)):
            ref[:, b * BLK : (b + 1) * BLK] = block

    for copy in copies[:2]:
        copy.wait()

    batch = 2 * chunk

    def transform():
        spec[...] = jnp.dot(
            seg[...], table[...], preferred_element_type=jnp.float32
        ) * (1.0 / math.sqrt(WIN))

    def single_window(slot, jitter, blocks_at):
        @pl.loop(0, stations // batch)
        def _(step):
            start = step * batch

            @pl.loop(0, batch // ROWS, unroll=4)
            def _(g):
                row = pl.multiple_of(start + g * ROWS, ROWS)
                write_segment(
                    blocks_at(row), jitter, taper, seg, pl.multiple_of(g * ROWS, ROWS)
                )

            transform()

            @pl.loop(0, batch // ROWS, unroll=4)
            def _(g):
                re, im = whiten_rows(spec, pl.multiple_of(g * ROWS, ROWS))
                row = pl.multiple_of(start + g * ROWS, ROWS)
                white[slot, pl.ds(row, ROWS), :NF] = re
                white[slot, pl.ds(row, ROWS), NF:] = im

    def swap(which, slot, depth):
        result = []
        for delta in range(1, n_sta):
            rows = CAP if min(delta, n_sta - delta) <= 1 else FAR_ROWS
            partner = (me + delta) % n_sta
            result.append(
                pltpu.make_async_remote_copy(
                    src_ref=outgoing.at[
                        pl.ds(slot, depth), pl.ds(pl.multiple_of(partner * CAP, CAP), rows)
                    ],
                    dst_ref=incoming.at[
                        pl.ds(slot, depth), pl.ds(pl.multiple_of(me * CAP, CAP), rows)
                    ],
                    send_sem=swap_send_sem.at[which, delta],
                    recv_sem=swap_recv_sem.at[which, delta],
                    device_id={"sta": partner},
                    device_id_type=MESH,
                )
            )
        return result

    def start_swap(which, slot, depth):
        for w in range(slot, slot + depth):
            outgoing[w] = jnp.dot(
                pick_send[...], white[w], preferred_element_type=jnp.float32
            ).astype(jnp.bfloat16)
        for copy in swap(which, slot, depth):
            copy.start()
        mine = pl.ds(pl.multiple_of(me * CAP, CAP), CAP)
        for w in range(slot, slot + depth):
            incoming[w, mine] = outgoing[w, mine]

    def end_swap(which, slot, depth):
        for copy in swap(which, slot, depth):
            copy.wait()

    def gather_first(w):
        first_rows[w] = jnp.dot(
            pick_first[...], white[w], preferred_element_type=jnp.float32
        ).astype(jnp.bfloat16)

    part = min(pairs, 256)
    width = 256

    def add_cross(windows, fresh, final):
        @pl.loop(0, pairs // part)
        def _(p):
            rows = pl.ds(pl.multiple_of(p * part, part), part)
            for b in range(NF // width):
                rcol = slice(b * width, (b + 1) * width)
                icol = slice(NF + b * width, NF + (b + 1) * width)
                real = None if fresh else cross_sum[rows, rcol]
                imag = None if fresh else cross_sum[rows, icol]
                for w in windows:
                    fr = first_rows[w, rows, rcol].astype(jnp.float32)
                    fi = first_rows[w, rows, icol].astype(jnp.float32)
                    sr = jnp.dot(
                        pick_second[rows], incoming[w, :, rcol],
                        preferred_element_type=jnp.float32,
                    )
                    si = jnp.dot(
                        pick_second[rows], incoming[w, :, icol],
                        preferred_element_type=jnp.float32,
                    )
                    new_real = fr * sr + fi * si
                    new_imag = fi * sr - fr * si
                    real = new_real if real is None else real + new_real
                    imag = new_imag if imag is None else imag + new_imag
                if final:
                    cross[rows, rcol] = real.astype(jnp.bfloat16)
                    cross[rows, icol] = imag.astype(jnp.bfloat16)
                else:
                    cross_sum[rows, rcol] = real
                    cross_sum[rows, icol] = imag

    single_window(0, offsets[0], lambda row: load_blocks(own, row, 0, 24))
    start_swap(0, 0, 1)

    @pl.when(is_last)
    def _():
        single_window(
            3,
            offsets[2] - 2 * STEP,
            lambda row: load_blocks(own, row, 16, 8)
            + [jnp.zeros((ROWS, BLK), jnp.float32)] * 16,
        )
        start_swap(2, 3, 1)

    gather_first(0)
    end_swap(0, 0, 1)
    add_cross((0,), True, False)

    @pl.when(is_last)
    def _():
        gather_first(3)
        end_swap(2, 3, 1)
        add_cross((3,), False, False)

    @pl.when(has_prev)
    def _():
        offset_up.wait_recv()

    jitter_1 = offsets[1] - STEP
    jitter_2 = offset_recv[0, 0] - 2 * STEP
    keep = jnp.where(has_prev, 1.0, 0.0).astype(jnp.float32)

    @pl.loop(0, CHUNKS)
    def _(c):
        @pl.when(has_prev)
        def _():
            rim_up(c).wait_recv()

        @pl.when(has_next)
        def _():
            rim_down(c).wait_recv()

        start = c * chunk

        @pl.loop(0, chunk // ROWS, unroll=2)
        def _(g):
            row = pl.multiple_of(start + g * ROWS, ROWS)
            at = pl.multiple_of(g * ROWS, ROWS)
            write_segment(
                load_blocks(own, row, 8, 16) + load_blocks(rim_next, row, 0, 8),
                jitter_1, taper, seg, at,
            )
            write_segment(
                load_blocks(rim_prev, row, 0, 8) + load_blocks(own, row, 0, 16),
                jitter_2, taper, seg, pl.multiple_of(chunk + g * ROWS, ROWS),
            )

        transform()

        @pl.loop(0, chunk // ROWS, unroll=2)
        def _(g):
            row = pl.multiple_of(start + g * ROWS, ROWS)
            re, im = whiten_rows(spec, pl.multiple_of(g * ROWS, ROWS))
            white[1, pl.ds(row, ROWS), :NF] = re
            white[1, pl.ds(row, ROWS), NF:] = im
            re, im = whiten_rows(spec, pl.multiple_of(chunk + g * ROWS, ROWS))
            white[2, pl.ds(row, ROWS), :NF] = (re * keep).astype(jnp.bfloat16)
            white[2, pl.ds(row, ROWS), NF:] = (im * keep).astype(jnp.bfloat16)

    start_swap(1, 1, 2)
    gather_first(1)
    gather_first(2)
    copies[2].wait()
    end_swap(1, 1, 2)
    add_cross((1, 2), False, True)

    span = pairs // PIECES

    def share(c, piece):
        return lax.dot_general(
            lags[pl.ds(pl.multiple_of(c * lag_rows, lag_rows), lag_rows)],
            cross[pl.ds(pl.multiple_of(piece * span, span), span)],
            (((1,), (1,)), ((), ())),
            preferred_element_type=jnp.float32,
        )

    def up(index):
        return pltpu.make_async_remote_copy(
            src_ref=up_send.at[index],
            dst_ref=up_recv.at[index],
            send_sem=up_send_sem.at[index],
            recv_sem=up_recv_sem.at[index],
            device_id={"tm": tm + 1},
            device_id_type=MESH,
        )

    def down(index):
        return pltpu.make_async_remote_copy(
            src_ref=down_send.at[index],
            dst_ref=down_recv.at[index],
            send_sem=down_send_sem.at[index],
            recv_sem=down_recv_sem.at[index],
            device_id={"tm": tm - 1},
            device_id_type=MESH,
        )

    @pl.loop(0, (n_tm - 1) * PIECES)
    def _(t):
        up_item = t - tm
        up_chunk = n_tm - 1 - up_item // PIECES
        up_piece = up_item % PIECES

        @pl.when((up_item >= 0) & (up_item < (n_tm - 1 - tm) * PIECES))
        def _():
            index = up_chunk * PIECES + up_piece
            own_share = share(up_chunk, up_piece)

            @pl.when(has_prev)
            def _():
                up(index).wait_recv()
                up_send[index] = (own_share + up_recv[index].astype(jnp.float32)).astype(
                    jnp.bfloat16
                )

            @pl.when(tm == 0)
            def _():
                up_send[index] = own_share.astype(jnp.bfloat16)

            up(index).start()

        down_item = t - (n_tm - 1 - tm)
        down_chunk = down_item // PIECES
        down_piece = down_item % PIECES

        @pl.when((down_item >= 0) & (down_item < tm * PIECES))
        def _():
            index = down_chunk * PIECES + down_piece
            own_share = share(down_chunk, down_piece)

            @pl.when(has_next)
            def _():
                down(index).wait_recv()
                down_send[index] = (own_share + down_recv[index].astype(jnp.float32)).astype(
                    jnp.bfloat16
                )

            @pl.when(is_last)
            def _():
                down_send[index] = own_share.astype(jnp.bfloat16)

            down(index).start()

    scaling = 1.0 / math.sqrt(NF * 3 * n_tm)
    for piece in range(PIECES):
        index = tm * PIECES + piece
        columns = slice(piece * span, (piece + 1) * span)
        out[:, columns] = share(tm, piece) * scaling

    for piece in range(PIECES):
        index = tm * PIECES + piece
        columns = slice(piece * span, (piece + 1) * span)

        @pl.when(has_prev)
        def _():
            up(index).wait_recv()
            out[:, columns] += up_recv[index].astype(jnp.float32) * scaling

        @pl.when(has_next)
        def _():
            down(index).wait_recv()
            out[:, columns] += down_recv[index].astype(jnp.float32) * scaling

    @pl.when(has_next)
    def _():
        offset_up.wait_send()

    for c in range(CHUNKS):

        @pl.when(has_next)
        def _():
            rim_up(c).wait_send()

        @pl.when(has_prev)
        def _():
            rim_down(c).wait_send()

    @pl.loop(0, n_tm * PIECES)
    def _(index):
        @pl.when(index >= (tm + 1) * PIECES)
        def _():
            up(index).wait_send()

        @pl.when(index < tm * PIECES)
        def _():
            down(index).wait_send()


def on_device(n_tm, n_sta, traces, offsets, pair_first, pair_slot, send_rows):
    stations = traces.shape[0]
    pairs = pair_first.shape[0]
    slots = n_sta * CAP
    lag_rows = NL // n_tm
    chunk = stations // CHUNKS
    items = n_tm * PIECES
    bf16, f32 = jnp.bfloat16, jnp.float32
    vmem = pl.BlockSpec(memory_space=pltpu.VMEM)
    smem = pl.BlockSpec(memory_space=pltpu.SMEM)
    hbm = pl.BlockSpec(memory_space=pl.ANY)
    dma = pltpu.SemaphoreType.DMA
    strip = pltpu.VMEM((items, lag_rows, pairs // PIECES), bf16)
    return pl.pallas_call(
        functools.partial(kernel, n_tm, n_sta),
        out_shape=jax.ShapeDtypeStruct((lag_rows, pairs), f32),
        in_specs=[smem, vmem, vmem, vmem, vmem, hbm, hbm, hbm],
        out_specs=vmem,
        scratch_shapes=[
            pltpu.VMEM((stations, TB), bf16),
            pltpu.VMEM((stations, STEP), bf16),
            pltpu.VMEM((stations, STEP), bf16),
            pltpu.VMEM((WIN, 2 * NF), bf16),
            pltpu.VMEM((NL, 2 * NF), bf16),
            pltpu.VMEM((2 * chunk, WIN), bf16),
            pltpu.VMEM((2 * chunk, 2 * NF), f32),
            pltpu.VMEM((4, stations, 2 * NF), bf16),
            pltpu.VMEM((4, slots, 2 * NF), bf16),
            pltpu.VMEM((4, slots, 2 * NF), bf16),
            pltpu.VMEM((pairs, stations), bf16),
            pltpu.VMEM((pairs, slots), bf16),
            pltpu.VMEM((slots, stations), bf16),
            pltpu.VMEM((4, pairs, 2 * NF), bf16),
            pltpu.VMEM((pairs, 2 * NF), f32),
            pltpu.VMEM((pairs, 2 * NF), bf16),
            strip,
            strip,
            strip,
            strip,
            pltpu.VMEM((8, BLK), jnp.int32),
            pltpu.VMEM((8, BLK), jnp.int32),
            dma((3,)),
            dma((2, CHUNKS)),
            dma((2, CHUNKS)),
            dma((2,)),
            dma((3, n_sta)),
            dma((3, n_sta)),
            dma((items,)),
            dma((items,)),
            dma((items,)),
            dma((items,)),
        ],
        compiler_params=pltpu.CompilerParams(
            collective_id=0, has_side_effects=True, vmem_limit_bytes=56 * 1024 * 1024
        ),
    )(
        offsets,
        pair_first.reshape(1, pairs),
        pair_slot.reshape(1, pairs),
        send_rows,
        jnp.asarray(taper_table()),
        traces,
        jnp.asarray(dft_table()),
        jnp.asarray(lag_table()),
    )


def solution(mesh):
    in_specs = (P("sta", ("day", "tm")), P(("day", "tm")), P("sta"), P("sta"), P("sta", None))
    out_specs = P(("day", "tm"), "sta")
    return jax.shard_map(
        functools.partial(on_device, mesh.shape["tm"], mesh.shape["sta"]),
        mesh=mesh,
        in_specs=in_specs,
        out_specs=out_specs,
        check_vma=False,
    )
```

```python
import functools
import math

import jax
import jax.numpy as jnp
import numpy as np
from jax import lax
from jax.experimental import pallas as pl
from jax.experimental.pallas import tpu as pltpu
from jax.sharding import PartitionSpec as P

WIN = 2048
NF = 512
NL = 1024
STEP = 1024
TB = 3072
CAP = 32
FAR_ROWS = 16
FLOOR = 0.1
CHUNKS = 4
PIECES = 2
BLK = 128
ROWS = 16
MESH = pl.DeviceIdType.MESH


def taper_table():
    n = np.arange(WIN, dtype=np.float64)
    return (0.5 - 0.5 * np.cos(2.0 * np.pi * n / WIN)).astype(np.float32)[None, :]


def dft_table():
    n = np.arange(WIN)[:, None]
    k = np.arange(NF)[None, :] + 1
    angle = (n * k % WIN) * (2.0 * np.pi / WIN)
    return np.concatenate([np.cos(angle), -np.sin(angle)], axis=1).astype(jnp.bfloat16)


def lag_table():
    t = np.arange(NL)[:, None] - NL // 2
    k = np.arange(NF)[None, :] + 1
    angle = (t * k % WIN) * (2.0 * np.pi / WIN)
    return np.concatenate([np.cos(angle), -np.sin(angle)], axis=1).astype(jnp.bfloat16)


def shifted(blocks, jitter):
    quotient = jitter // BLK
    rest = jitter % BLK
    for bit, count in ((8, 24), (4, 20), (2, 18), (1, 17)):
        on = (quotient // bit) % 2 == 1
        blocks = [
            jnp.where(on, blocks[i + bit], blocks[i]) if i + bit < len(blocks) else blocks[i]
            for i in range(count)
        ]
    turn = (BLK - rest) % BLK
    rolled = [pltpu.roll(b, turn, 1) for b in blocks]
    lane = lax.broadcasted_iota(jnp.int32, blocks[0].shape, 1)
    keep = lane < BLK - rest
    return [jnp.where(keep, rolled[i], rolled[i + 1]) for i in range(WIN // BLK)]


def write_segment(blocks, jitter, taper, seg, row):
    values = [v.astype(jnp.float32) for v in shifted(blocks, jitter)]
    sums = values
    while len(sums) > 1:
        sums = [a + b for a, b in zip(sums[::2], sums[1::2])]
    total = sums[0]
    mean = jnp.sum(total, axis=1, keepdims=True) * (1.0 / WIN)
    for i, v in enumerate(values):
        columns = slice(i * BLK, (i + 1) * BLK)
        seg[pl.ds(row, ROWS), columns] = ((v - mean) * taper[:, columns]).astype(jnp.bfloat16)


def load_blocks(ref, row, first, count):
    return [
        ref[pl.ds(row, ROWS), i * BLK : (i + 1) * BLK]
        for i in range(first, first + count)
    ]


def whiten_rows(spec, row):
    re = spec[pl.ds(row, ROWS), :NF]
    im = spec[pl.ds(row, ROWS), NF:]
    amplitude = jnp.sqrt(re * re + im * im + 1e-06)
    wide = jnp.concatenate([amplitude, jnp.zeros((ROWS, BLK), jnp.float32)], axis=1)
    width = NF + BLK
    pair = wide + pltpu.roll(wide, 1, 1)
    five = wide + pltpu.roll(pair, 1, 1) + pltpu.roll(pair, width - 2, 1)
    inverse = 1.0 / jnp.maximum(five[:, :NF] * (1.0 / 5.0), FLOOR)
    return (re * inverse).astype(jnp.bfloat16), (im * inverse).astype(jnp.bfloat16)


def kernel(
    n_tm, n_sta,
    offsets, pair_first, pair_slot, send_rows, taper, traces, table_hbm, lag_hbm,
    out,
    own, rim_prev, rim_next, table, lags, seg, spec, white, outgoing, incoming,
    pick_first, pick_second, pick_send, first_rows, cross_sum, cross,
    up_send, up_recv, down_send, down_recv, offset_send, offset_recv,
    local_sem, rim_send_sem, rim_recv_sem, offset_sem, swap_send_sem, swap_recv_sem,
    up_send_sem, up_recv_sem, down_send_sem, down_recv_sem,
):
    stations = own.shape[0]
    pairs = out.shape[1]
    lag_rows = out.shape[0]
    slots = n_sta * CAP
    chunk = stations // CHUNKS
    tm = lax.axis_index("tm")
    me = lax.axis_index("sta")
    has_prev = tm > 0
    has_next = tm < n_tm - 1
    is_last = tm == n_tm - 1

    copies = [
        pltpu.make_async_copy(traces, own, local_sem.at[0]),
        pltpu.make_async_copy(table_hbm, table, local_sem.at[1]),
        pltpu.make_async_copy(lag_hbm, lags, local_sem.at[2]),
    ]
    for copy in copies:
        copy.start()

    incoming[...] = jnp.zeros_like(incoming)
    offset_send[...] = jnp.full(offset_send.shape, offsets[2], jnp.int32)

    @pl.when(tm == 0)
    def _():
        rim_prev[...] = jnp.zeros_like(rim_prev)
        offset_recv[...] = jnp.full(offset_recv.shape, 2 * STEP, jnp.int32)

    @pl.when(is_last)
    def _():
        rim_next[...] = jnp.zeros_like(rim_next)

    barrier = pltpu.get_barrier_semaphore()
    for delta in range(1, n_sta):
        pl.semaphore_signal(
            barrier, inc=1, device_id={"sta": (me + delta) % n_sta}, device_id_type=MESH
        )

    @pl.when(has_prev)
    def _():
        pl.semaphore_signal(barrier, inc=1, device_id={"tm": tm - 1}, device_id_type=MESH)

    @pl.when(has_next)
    def _():
        pl.semaphore_signal(barrier, inc=1, device_id={"tm": tm + 1}, device_id_type=MESH)

    greeted = n_sta - 1 + has_prev.astype(jnp.int32) + has_next.astype(jnp.int32)
    pl.semaphore_wait(barrier, greeted)

    def rim_up(c):
        rows = pl.ds(c * chunk, chunk)
        return pltpu.make_async_remote_copy(
            src_ref=traces.at[rows, pl.ds(TB - STEP, STEP)],
            dst_ref=rim_prev.at[rows],
            send_sem=rim_send_sem.at[0, c],
            recv_sem=rim_recv_sem.at[0, c],
            device_id={"tm": tm + 1},
            device_id_type=MESH,
        )

    def rim_down(c):
        rows = pl.ds(c * chunk, chunk)
        return pltpu.make_async_remote_copy(
            src_ref=traces.at[rows, pl.ds(0, STEP)],
            dst_ref=rim_next.at[rows],
            send_sem=rim_send_sem.at[1, c],
            recv_sem=rim_recv_sem.at[1, c],
            device_id={"tm": tm - 1},
            device_id_type=MESH,
        )

    offset_up = pltpu.make_async_remote_copy(
        src_ref=offset_send,
        dst_ref=offset_recv,
        send_sem=offset_sem.at[0],
        recv_sem=offset_sem.at[1],
        device_id={"tm": tm + 1},
        device_id_type=MESH,
    )

    @pl.when(has_next)
    def _():
        offset_up.start()

    for c in range(CHUNKS):

        @pl.when(has_next)
        def _():
            rim_up(c).start()

        @pl.when(has_prev)
        def _():
            rim_down(c).start()

    def one_hot(values, count, depth):
        spread = jnp.transpose(
            jnp.broadcast_to(values.astype(jnp.float32), (BLK, count))
        )
        lane = lax.broadcasted_iota(jnp.int32, (count, BLK), 1).astype(jnp.float32)
        return [
            (spread == lane + float(b * BLK)).astype(jnp.float32).astype(jnp.bfloat16)
            for b in range(depth // BLK)
        ]

    for ref, values, count, depth in (
        (pick_first, pair_first, pairs, stations),
        (pick_second, pair_slot, pairs, slots),
        (pick_send, send_rows, slots, stations),
    ):
        for b, block in enumerate(one_hot(values[...], count, depth)):
            ref[:, b * BLK : (b + 1) * BLK] = block

    for copy in copies[:2]:
        copy.wait()

    batch = stations

    def transform(count):
        spec[:count] = jnp.dot(
            seg[:count], table[...], preferred_element_type=jnp.float32
        ) * (1.0 / math.sqrt(WIN))

    def single_window(slot, jitter, blocks_at):
        @pl.loop(0, stations // batch)
        def _(step):
            start = step * batch

            @pl.loop(0, batch // ROWS, unroll=4)
            def _(g):
                row = pl.multiple_of(start + g * ROWS, ROWS)
                write_segment(
                    blocks_at(row), jitter, taper, seg, pl.multiple_of(g * ROWS, ROWS)
                )

            transform(batch)

            @pl.loop(0, batch // ROWS, unroll=4)
            def _(g):
                re, im = whiten_rows(spec, pl.multiple_of(g * ROWS, ROWS))
                row = pl.multiple_of(start + g * ROWS, ROWS)
                white[slot, pl.ds(row, ROWS), :NF] = re
                white[slot, pl.ds(row, ROWS), NF:] = im

    def swap(which, slot, depth):
        result = []
        for delta in range(1, n_sta):
            rows = CAP if min(delta, n_sta - delta) <= 1 else FAR_ROWS
            partner = (me + delta) % n_sta
            result.append(
                pltpu.make_async_remote_copy(
                    src_ref=outgoing.at[
                        pl.ds(slot, depth), pl.ds(pl.multiple_of(partner * CAP, CAP), rows)
                    ],
                    dst_ref=incoming.at[
                        pl.ds(slot, depth), pl.ds(pl.multiple_of(me * CAP, CAP), rows)
                    ],
                    send_sem=swap_send_sem.at[which, delta],
                    recv_sem=swap_recv_sem.at[which, delta],
                    device_id={"sta": partner},
                    device_id_type=MESH,
                )
            )
        return result

    def start_swap(which, slot, depth):
        for w in range(slot, slot + depth):
            outgoing[w] = jnp.dot(
                pick_send[...], white[w], preferred_element_type=jnp.float32
            ).astype(jnp.bfloat16)
        for copy in swap(which, slot, depth):
            copy.start()
        mine = pl.ds(pl.multiple_of(me * CAP, CAP), CAP)
        for w in range(slot, slot + depth):
            incoming[w, mine] = outgoing[w, mine]

    def end_swap(which, slot, depth):
        for copy in swap(which, slot, depth):
            copy.wait()

    def gather_first(w):
        first_rows[w] = jnp.dot(
            pick_first[...], white[w], preferred_element_type=jnp.float32
        ).astype(jnp.bfloat16)

    part = pairs // PIECES
    width = 256

    def cross_part(p, windows, fresh, final):
        rows = pl.ds(pl.multiple_of(p * part, part), part)
        for b in range(NF // width):
            rcol = slice(b * width, (b + 1) * width)
            icol = slice(NF + b * width, NF + (b + 1) * width)
            real = None if fresh else cross_sum[rows, rcol]
            imag = None if fresh else cross_sum[rows, icol]
            for w in windows:
                fr = first_rows[w, rows, rcol].astype(jnp.float32)
                fi = first_rows[w, rows, icol].astype(jnp.float32)
                sr = jnp.dot(
                    pick_second[rows], incoming[w, :, rcol],
                    preferred_element_type=jnp.float32,
                )
                si = jnp.dot(
                    pick_second[rows], incoming[w, :, icol],
                    preferred_element_type=jnp.float32,
                )
                new_real = fr * sr + fi * si
                new_imag = fi * sr - fr * si
                real = new_real if real is None else real + new_real
                imag = new_imag if imag is None else imag + new_imag
            if final:
                cross[rows, rcol] = real.astype(jnp.bfloat16)
                cross[rows, icol] = imag.astype(jnp.bfloat16)
            else:
                cross_sum[rows, rcol] = real
                cross_sum[rows, icol] = imag

    def add_cross(windows, fresh):
        @pl.loop(0, PIECES)
        def _(p):
            cross_part(p, windows, fresh, False)

    single_window(0, offsets[0], lambda row: load_blocks(own, row, 0, 24))
    start_swap(0, 0, 1)

    @pl.when(is_last)
    def _():
        single_window(
            3,
            offsets[2] - 2 * STEP,
            lambda row: load_blocks(own, row, 16, 8)
            + [jnp.zeros((ROWS, BLK), jnp.bfloat16)] * 16,
        )
        start_swap(2, 3, 1)

    gather_first(0)
    end_swap(0, 0, 1)
    add_cross((0,), True)

    @pl.when(is_last)
    def _():
        gather_first(3)
        end_swap(2, 3, 1)
        add_cross((3,), False)

    @pl.when(has_prev)
    def _():
        offset_up.wait_recv()

    jitter_1 = offsets[1] - STEP
    jitter_2 = offset_recv[0, 0] - 2 * STEP
    keep = jnp.where(has_prev, 1.0, 0.0).astype(jnp.float32)

    @pl.loop(0, CHUNKS)
    def _(c):
        @pl.when(has_prev)
        def _():
            rim_up(c).wait_recv()

        @pl.when(has_next)
        def _():
            rim_down(c).wait_recv()

        start = c * chunk

        @pl.loop(0, chunk // ROWS, unroll=2)
        def _(g):
            row = pl.multiple_of(start + g * ROWS, ROWS)
            at = pl.multiple_of(g * ROWS, ROWS)
            write_segment(
                load_blocks(own, row, 8, 16) + load_blocks(rim_next, row, 0, 8),
                jitter_1, taper, seg, at,
            )
            write_segment(
                load_blocks(rim_prev, row, 0, 8) + load_blocks(own, row, 0, 16),
                jitter_2, taper, seg, pl.multiple_of(chunk + g * ROWS, ROWS),
            )

        transform(2 * chunk)

        @pl.loop(0, chunk // ROWS, unroll=4)
        def _(g):
            row = pl.multiple_of(start + g * ROWS, ROWS)
            re, im = whiten_rows(spec, pl.multiple_of(g * ROWS, ROWS))
            white[1, pl.ds(row, ROWS), :NF] = re
            white[1, pl.ds(row, ROWS), NF:] = im
            re, im = whiten_rows(spec, pl.multiple_of(chunk + g * ROWS, ROWS))
            white[2, pl.ds(row, ROWS), :NF] = (re * keep).astype(jnp.bfloat16)
            white[2, pl.ds(row, ROWS), NF:] = (im * keep).astype(jnp.bfloat16)

    start_swap(1, 1, 2)
    gather_first(1)
    gather_first(2)
    copies[2].wait()
    end_swap(1, 1, 2)

    span = pairs // PIECES

    def share(c, piece):
        return lax.dot_general(
            lags[pl.ds(pl.multiple_of(c * lag_rows, lag_rows), lag_rows)],
            cross[pl.ds(pl.multiple_of(piece * span, span), span)],
            (((1,), (1,)), ((), ())),
            preferred_element_type=jnp.float32,
        )

    def up(index):
        return pltpu.make_async_remote_copy(
            src_ref=up_send.at[index],
            dst_ref=up_recv.at[index],
            send_sem=up_send_sem.at[index],
            recv_sem=up_recv_sem.at[index],
            device_id={"tm": tm + 1},
            device_id_type=MESH,
        )

    def down(index):
        return pltpu.make_async_remote_copy(
            src_ref=down_send.at[index],
            dst_ref=down_recv.at[index],
            send_sem=down_send_sem.at[index],
            recv_sem=down_recv_sem.at[index],
            device_id={"tm": tm - 1},
            device_id_type=MESH,
        )

    @pl.loop(0, (n_tm - 1) * PIECES)
    def _(t):
        @pl.when(t < PIECES)
        def _():
            cross_part(t, (1, 2), False, True)

        up_item = t - tm
        up_chunk = n_tm - 1 - up_item // PIECES
        up_piece = up_item % PIECES

        @pl.when((up_item >= 0) & (up_item < (n_tm - 1 - tm) * PIECES))
        def _():
            index = up_chunk * PIECES + up_piece
            own_share = share(up_chunk, up_piece)

            @pl.when(has_prev)
            def _():
                up(index).wait_recv()
                up_send[index] = (own_share + up_recv[index].astype(jnp.float32)).astype(
                    jnp.bfloat16
                )

            @pl.when(tm == 0)
            def _():
                up_send[index] = own_share.astype(jnp.bfloat16)

            up(index).start()

        down_item = t - (n_tm - 1 - tm)
        down_chunk = down_item // PIECES
        down_piece = down_item % PIECES

        @pl.when((down_item >= 0) & (down_item < tm * PIECES))
        def _():
            index = down_chunk * PIECES + down_piece
            own_share = share(down_chunk, down_piece)

            @pl.when(has_next)
            def _():
                down(index).wait_recv()
                down_send[index] = (own_share + down_recv[index].astype(jnp.float32)).astype(
                    jnp.bfloat16
                )

            @pl.when(is_last)
            def _():
                down_send[index] = own_share.astype(jnp.bfloat16)

            down(index).start()

    scaling = 1.0 / math.sqrt(NF * 3 * n_tm)
    for piece in range(PIECES):
        index = tm * PIECES + piece
        columns = slice(piece * span, (piece + 1) * span)
        out[:, columns] = share(tm, piece) * scaling

    for piece in range(PIECES):
        index = tm * PIECES + piece
        columns = slice(piece * span, (piece + 1) * span)

        @pl.when(has_prev)
        def _():
            up(index).wait_recv()
            out[:, columns] += up_recv[index].astype(jnp.float32) * scaling

        @pl.when(has_next)
        def _():
            down(index).wait_recv()
            out[:, columns] += down_recv[index].astype(jnp.float32) * scaling

    @pl.when(has_next)
    def _():
        offset_up.wait_send()

    for c in range(CHUNKS):

        @pl.when(has_next)
        def _():
            rim_up(c).wait_send()

        @pl.when(has_prev)
        def _():
            rim_down(c).wait_send()

    @pl.loop(0, n_tm * PIECES)
    def _(index):
        @pl.when(index >= (tm + 1) * PIECES)
        def _():
            up(index).wait_send()

        @pl.when(index < tm * PIECES)
        def _():
            down(index).wait_send()


def on_device(n_tm, n_sta, traces, offsets, pair_first, pair_slot, send_rows):
    stations = traces.shape[0]
    pairs = pair_first.shape[0]
    slots = n_sta * CAP
    lag_rows = NL // n_tm
    chunk = stations // CHUNKS
    items = n_tm * PIECES
    bf16, f32 = jnp.bfloat16, jnp.float32
    vmem = pl.BlockSpec(memory_space=pltpu.VMEM)
    smem = pl.BlockSpec(memory_space=pltpu.SMEM)
    hbm = pl.BlockSpec(memory_space=pl.ANY)
    dma = pltpu.SemaphoreType.DMA
    strip = pltpu.VMEM((items, lag_rows, pairs // PIECES), bf16)
    return pl.pallas_call(
        functools.partial(kernel, n_tm, n_sta),
        out_shape=jax.ShapeDtypeStruct((lag_rows, pairs), f32),
        in_specs=[smem, vmem, vmem, vmem, vmem, hbm, hbm, hbm],
        out_specs=vmem,
        scratch_shapes=[
            pltpu.VMEM((stations, TB), bf16),
            pltpu.VMEM((stations, STEP), bf16),
            pltpu.VMEM((stations, STEP), bf16),
            pltpu.VMEM((WIN, 2 * NF), bf16),
            pltpu.VMEM((NL, 2 * NF), bf16),
            pltpu.VMEM((stations, WIN), bf16),
            pltpu.VMEM((stations, 2 * NF), f32),
            pltpu.VMEM((4, stations, 2 * NF), bf16),
            pltpu.VMEM((4, slots, 2 * NF), bf16),
            pltpu.VMEM((4, slots, 2 * NF), bf16),
            pltpu.VMEM((pairs, stations), bf16),
            pltpu.VMEM((pairs, slots), bf16),
            pltpu.VMEM((slots, stations), bf16),
            pltpu.VMEM((4, pairs, 2 * NF), bf16),
            pltpu.VMEM((pairs, 2 * NF), f32),
            pltpu.VMEM((pairs, 2 * NF), bf16),
            strip,
            strip,
            strip,
            strip,
            pltpu.VMEM((8, BLK), jnp.int32),
            pltpu.VMEM((8, BLK), jnp.int32),
            dma((3,)),
            dma((2, CHUNKS)),
            dma((2, CHUNKS)),
            dma((2,)),
            dma((3, n_sta)),
            dma((3, n_sta)),
            dma((items,)),
            dma((items,)),
            dma((items,)),
            dma((items,)),
        ],
        compiler_params=pltpu.CompilerParams(
            collective_id=0, has_side_effects=True, vmem_limit_bytes=56 * 1024 * 1024
        ),
    )(
        offsets,
        pair_first.reshape(1, pairs),
        pair_slot.reshape(1, pairs),
        send_rows,
        jnp.asarray(taper_table()),
        traces,
        jnp.asarray(dft_table()),
        jnp.asarray(lag_table()),
    )


def solution(mesh):
    in_specs = (P("sta", ("day", "tm")), P(("day", "tm")), P("sta"), P("sta"), P("sta", None))
    out_specs = P(("day", "tm"), "sta")
    return jax.shard_map(
        functools.partial(on_device, mesh.shape["tm"], mesh.shape["sta"]),
        mesh=mesh,
        in_specs=in_specs,
        out_specs=out_specs,
        check_vma=False,
    )
```

```python
import functools
import math

import jax
import jax.numpy as jnp
import numpy as np
from jax import lax
from jax.experimental import pallas as pl
from jax.experimental.pallas import tpu as pltpu
from jax.sharding import PartitionSpec as P

WIN = 2048
NF = 512
NL = 1024
STEP = 1024
TB = 3072
CAP = 32
FAR_ROWS = 16
FLOOR = 0.1
CHUNKS = 4
PIECES = 2
BLK = 128
ROWS = 16
MESH = pl.DeviceIdType.MESH


def taper_table():
    n = np.arange(WIN, dtype=np.float64)
    return (0.5 - 0.5 * np.cos(2.0 * np.pi * n / WIN)).astype(np.float32)[None, :]


def dft_table():
    n = np.arange(WIN)[:, None]
    k = np.arange(NF)[None, :] + 1
    angle = (n * k % WIN) * (2.0 * np.pi / WIN)
    return np.concatenate([np.cos(angle), -np.sin(angle)], axis=1).astype(jnp.bfloat16)


def lag_table():
    t = np.arange(NL)[:, None] - NL // 2
    k = np.arange(NF)[None, :] + 1
    angle = (t * k % WIN) * (2.0 * np.pi / WIN)
    return np.concatenate([np.cos(angle), -np.sin(angle)], axis=1).astype(jnp.bfloat16)


def shifted(blocks, jitter):
    quotient = jitter // BLK
    rest = jitter % BLK
    for bit, count in ((8, 24), (4, 20), (2, 18), (1, 17)):
        on = (quotient // bit) % 2 == 1
        blocks = [
            jnp.where(on, blocks[i + bit], blocks[i]) if i + bit < len(blocks) else blocks[i]
            for i in range(count)
        ]
    turn = (BLK - rest) % BLK
    rolled = [pltpu.roll(b, turn, 1) for b in blocks]
    lane = lax.broadcasted_iota(jnp.int32, blocks[0].shape, 1)
    keep = lane < BLK - rest
    return [jnp.where(keep, rolled[i], rolled[i + 1]) for i in range(WIN // BLK)]


def write_segment(blocks, jitter, taper, seg, row):
    values = [v.astype(jnp.float32) for v in shifted(blocks, jitter)]
    sums = values
    while len(sums) > 1:
        sums = [a + b for a, b in zip(sums[::2], sums[1::2])]
    total = sums[0]
    mean = jnp.sum(total, axis=1, keepdims=True) * (1.0 / WIN)
    for i, v in enumerate(values):
        columns = slice(i * BLK, (i + 1) * BLK)
        seg[pl.ds(row, ROWS), columns] = ((v - mean) * taper[:, columns]).astype(jnp.bfloat16)


def load_blocks(ref, row, first, count):
    return [
        ref[pl.ds(row, ROWS), i * BLK : (i + 1) * BLK]
        for i in range(first, first + count)
    ]


def whiten_rows(spec, row):
    re = spec[pl.ds(row, ROWS), :NF]
    im = spec[pl.ds(row, ROWS), NF:]
    amplitude = jnp.sqrt(re * re + im * im + 1e-06)
    wide = jnp.concatenate([amplitude, jnp.zeros((ROWS, BLK), jnp.float32)], axis=1)
    width = NF + BLK
    pair = wide + pltpu.roll(wide, 1, 1)
    five = wide + pltpu.roll(pair, 1, 1) + pltpu.roll(pair, width - 2, 1)
    inverse = 1.0 / jnp.maximum(five[:, :NF] * (1.0 / 5.0), FLOOR)
    return (re * inverse).astype(jnp.bfloat16), (im * inverse).astype(jnp.bfloat16)


def kernel(
    n_tm, n_sta,
    offsets, pair_first, pair_slot, send_rows, taper, traces, table_hbm, lag_hbm,
    out,
    raw, own, rim_prev, rim_next, table, lags, seg, spec, white, outgoing, incoming,
    pick_first, pick_second, pick_send, order, first_at, send_at, second_rows, cross_sum, cross,
    up_send, up_recv, down_send, down_recv, offset_send, offset_recv,
    local_sem, rim_send_sem, rim_recv_sem, offset_sem, swap_send_sem, swap_recv_sem,
    up_send_sem, up_recv_sem, down_send_sem, down_recv_sem,
):
    stations = own.shape[0]
    pairs = out.shape[1]
    lag_rows = out.shape[0]
    slots = n_sta * CAP
    chunk = stations // CHUNKS
    half = chunk // 2
    early = slots <= chunk
    tm = lax.axis_index("tm")
    me = lax.axis_index("sta")
    has_prev = tm > 0
    has_next = tm < n_tm - 1
    is_last = tm == n_tm - 1

    copies = [
        pltpu.make_async_copy(traces, raw, local_sem.at[0]),
        pltpu.make_async_copy(table_hbm, table, local_sem.at[1]),
        pltpu.make_async_copy(lag_hbm, lags, local_sem.at[2]),
    ]
    for copy in copies:
        copy.start()

    incoming[...] = jnp.zeros_like(incoming)
    offset_send[...] = jnp.full(offset_send.shape, offsets[2], jnp.int32)

    @pl.when(tm == 0)
    def _():
        rim_prev[...] = jnp.zeros_like(rim_prev)
        offset_recv[...] = jnp.full(offset_recv.shape, 2 * STEP, jnp.int32)

    @pl.when(is_last)
    def _():
        rim_next[...] = jnp.zeros_like(rim_next)

    barrier = pltpu.get_barrier_semaphore()
    for delta in range(1, n_sta):
        pl.semaphore_signal(
            barrier, inc=1, device_id={"sta": (me + delta) % n_sta}, device_id_type=MESH
        )

    @pl.when(has_prev)
    def _():
        pl.semaphore_signal(barrier, inc=1, device_id={"tm": tm - 1}, device_id_type=MESH)

    @pl.when(has_next)
    def _():
        pl.semaphore_signal(barrier, inc=1, device_id={"tm": tm + 1}, device_id_type=MESH)

    def rim_rows(c):
        if isinstance(c, int) and c >= CHUNKS - 1:
            return pl.ds((CHUNKS - 1) * chunk + (c - CHUNKS + 1) * half, half)
        return pl.ds(c * chunk, chunk)

    def rim_up(c):
        rows = rim_rows(c)
        return pltpu.make_async_remote_copy(
            src_ref=own.at[rows, pl.ds(TB - STEP, STEP)],
            dst_ref=rim_prev.at[rows],
            send_sem=rim_send_sem.at[0, c],
            recv_sem=rim_recv_sem.at[0, c],
            device_id={"tm": tm + 1},
            device_id_type=MESH,
        )

    def rim_down(c):
        rows = rim_rows(c)
        return pltpu.make_async_remote_copy(
            src_ref=own.at[rows, pl.ds(0, STEP)],
            dst_ref=rim_next.at[rows],
            send_sem=rim_send_sem.at[1, c],
            recv_sem=rim_recv_sem.at[1, c],
            device_id={"tm": tm - 1},
            device_id_type=MESH,
        )

    offset_up = pltpu.make_async_remote_copy(
        src_ref=offset_send,
        dst_ref=offset_recv,
        send_sem=offset_sem.at[0],
        recv_sem=offset_sem.at[1],
        device_id={"tm": tm + 1},
        device_id_type=MESH,
    )

    def one_hot(ref, values, depth):
        count = values.shape[1]
        spread = jnp.transpose(jnp.broadcast_to(values.astype(jnp.float32), (BLK, count)))
        lane = lax.broadcasted_iota(jnp.int32, (count, BLK), 1).astype(jnp.float32)
        for b in range(depth // BLK):
            ref[:, b * BLK : (b + 1) * BLK] = (
                (spread == lane + float(b * BLK)).astype(jnp.float32).astype(jnp.bfloat16)
            )

    one_hot(pick_send, send_rows[...], stations)
    hits = jnp.dot(
        jnp.ones((8, slots), jnp.bfloat16), pick_send[...], preferred_element_type=jnp.float32
    )
    chosen = hits > 0.5
    mark = chosen.astype(jnp.float32)
    from_row = lax.broadcasted_iota(jnp.int32, (stations, stations), 0)
    to_lane = lax.broadcasted_iota(jnp.int32, (stations, stations), 1)
    up_to = (from_row <= to_lane).astype(jnp.float32).astype(jnp.bfloat16)
    running = jnp.dot(mark.astype(jnp.bfloat16), up_to, preferred_element_type=jnp.float32)
    lane = lax.broadcasted_iota(jnp.int32, (8, stations), 1).astype(jnp.float32)
    total = jnp.sum(mark, axis=1, keepdims=True)
    place = jnp.where(chosen, running - 1.0, total + lane - running)
    order[...] = (
        (place[:1] == from_row.astype(jnp.float32)).astype(jnp.float32).astype(jnp.bfloat16)
    )

    copies[0].wait()

    def arrange(rows, columns):
        own[rows, columns] = jnp.dot(
            order[rows], raw[:, columns], preferred_element_type=jnp.float32
        ).astype(jnp.bfloat16)

    for c in range(CHUNKS + 1):
        arrange(rim_rows(c), slice(0, STEP))
        arrange(rim_rows(c), slice(TB - STEP, TB))

        if c == 0:
            greeted = n_sta - 1 + has_prev.astype(jnp.int32) + has_next.astype(jnp.int32)
            pl.semaphore_wait(barrier, greeted)

            @pl.when(has_next)
            def _():
                offset_up.start()

        @pl.when(has_next)
        def _():
            rim_up(c).start()

        @pl.when(has_prev)
        def _():
            rim_down(c).start()

    arrange(slice(0, stations), slice(STEP, TB - STEP))

    def in_order(ref):
        return lax.dot_general(
            ref[...], order[...], (((1,), (1,)), ((), ())),
            preferred_element_type=jnp.float32,
        ).astype(jnp.bfloat16)

    one_hot(pick_first, pair_first[...], stations)
    one_hot(pick_second, pair_slot[...], slots)
    first_at[...] = in_order(pick_first)
    send_at[...] = in_order(pick_send)
    copies[1].wait()

    batch = stations

    def transform(count):
        spec[:count] = jnp.dot(
            seg[:count], table[...], preferred_element_type=jnp.float32
        ) * (1.0 / math.sqrt(WIN))

    def single_window(slot, jitter, blocks_at):
        @pl.loop(0, stations // batch)
        def _(step):
            start = step * batch

            @pl.loop(0, batch // ROWS, unroll=4)
            def _(g):
                row = pl.multiple_of(start + g * ROWS, ROWS)
                write_segment(
                    blocks_at(row), jitter, taper, seg, pl.multiple_of(g * ROWS, ROWS)
                )

            transform(batch)

            @pl.loop(0, batch // ROWS, unroll=4)
            def _(g):
                re, im = whiten_rows(spec, pl.multiple_of(g * ROWS, ROWS))
                row = pl.multiple_of(start + g * ROWS, ROWS)
                white[slot, pl.ds(row, ROWS), :NF] = re
                white[slot, pl.ds(row, ROWS), NF:] = im

    def swap(which, slot, depth):
        result = []
        for delta in range(1, n_sta):
            rows = CAP if min(delta, n_sta - delta) <= 1 else FAR_ROWS
            partner = (me + delta) % n_sta
            result.append(
                pltpu.make_async_remote_copy(
                    src_ref=outgoing.at[
                        pl.ds(slot, depth), pl.ds(pl.multiple_of(partner * CAP, CAP), rows)
                    ],
                    dst_ref=incoming.at[
                        pl.ds(slot, depth), pl.ds(pl.multiple_of(me * CAP, CAP), rows)
                    ],
                    send_sem=swap_send_sem.at[which, delta],
                    recv_sem=swap_recv_sem.at[which, delta],
                    device_id={"sta": partner},
                    device_id_type=MESH,
                )
            )
        return result

    lead = min(slots, stations)

    def start_swap(which, slot, depth):
        for w in range(slot, slot + depth):
            outgoing[w] = jnp.dot(
                send_at[:, :lead], white[w, :lead], preferred_element_type=jnp.float32
            ).astype(jnp.bfloat16)
        for copy in swap(which, slot, depth):
            copy.start()
        mine = pl.ds(pl.multiple_of(me * CAP, CAP), CAP)
        for w in range(slot, slot + depth):
            incoming[w, mine] = outgoing[w, mine]

    def end_swap(which, slot, depth):
        for copy in swap(which, slot, depth):
            copy.wait()
        for w in range(slot, slot + depth):
            second_rows[w] = jnp.dot(
                pick_second[...], incoming[w], preferred_element_type=jnp.float32
            ).astype(jnp.bfloat16)

    part = pairs // PIECES
    width = 256

    def cross_part(p, windows, low, high, fresh=False, final=False):
        rows = pl.ds(pl.multiple_of(p * part, part), part)
        for b in range(NF // width):
            rcol = slice(b * width, (b + 1) * width)
            icol = slice(NF + b * width, NF + (b + 1) * width)
            real = None if fresh else cross_sum[rows, rcol]
            imag = None if fresh else cross_sum[rows, icol]
            for w in windows:
                fr, fi = [
                    jnp.dot(
                        first_at[rows, low:high], white[w, low:high, columns],
                        preferred_element_type=jnp.float32,
                    )
                    for columns in (rcol, icol)
                ]
                sr = second_rows[w, rows, rcol].astype(jnp.float32)
                si = second_rows[w, rows, icol].astype(jnp.float32)
                new_real = fr * sr + fi * si
                new_imag = fi * sr - fr * si
                real = new_real if real is None else real + new_real
                imag = new_imag if imag is None else imag + new_imag
            if final:
                cross[rows, rcol] = real.astype(jnp.bfloat16)
                cross[rows, icol] = imag.astype(jnp.bfloat16)
            else:
                cross_sum[rows, rcol] = real
                cross_sum[rows, icol] = imag

    def add_cross(windows, low, high, fresh=False):
        @pl.loop(0, PIECES)
        def _(p):
            cross_part(p, windows, low, high, fresh=fresh)

    single_window(0, offsets[0], lambda row: load_blocks(own, row, 0, 24))
    start_swap(0, 0, 1)

    @pl.when(is_last)
    def _():
        single_window(
            3,
            offsets[2] - 2 * STEP,
            lambda row: load_blocks(own, row, 16, 8)
            + [jnp.zeros((ROWS, BLK), jnp.bfloat16)] * 16,
        )
        start_swap(2, 3, 1)

    @pl.when(has_prev)
    def _():
        offset_up.wait_recv()

    jitter_1 = offsets[1] - STEP
    jitter_2 = offset_recv[0, 0] - 2 * STEP
    keep = jnp.where(has_prev, 1.0, 0.0).astype(jnp.float32)

    def two_windows(c, start, size):
        @pl.when(has_prev)
        def _():
            rim_up(c).wait_recv()

        @pl.when(has_next)
        def _():
            rim_down(c).wait_recv()

        @pl.loop(0, size // ROWS, unroll=2)
        def _(g):
            row = pl.multiple_of(start + g * ROWS, ROWS)
            at = pl.multiple_of(g * ROWS, ROWS)
            write_segment(
                load_blocks(own, row, 8, 16) + load_blocks(rim_next, row, 0, 8),
                jitter_1, taper, seg, at,
            )
            write_segment(
                load_blocks(rim_prev, row, 0, 8) + load_blocks(own, row, 0, 16),
                jitter_2, taper, seg, pl.multiple_of(size + g * ROWS, ROWS),
            )

        transform(2 * size)

        @pl.loop(0, size // ROWS, unroll=2)
        def _(g):
            row = pl.multiple_of(start + g * ROWS, ROWS)
            re, im = whiten_rows(spec, pl.multiple_of(g * ROWS, ROWS))
            white[1, pl.ds(row, ROWS), :NF] = re
            white[1, pl.ds(row, ROWS), NF:] = im
            re, im = whiten_rows(spec, pl.multiple_of(size + g * ROWS, ROWS))
            white[2, pl.ds(row, ROWS), :NF] = (re * keep).astype(jnp.bfloat16)
            white[2, pl.ds(row, ROWS), NF:] = (im * keep).astype(jnp.bfloat16)

    def finish_early_windows():
        end_swap(0, 0, 1)
        add_cross((0,), 0, stations, fresh=True)

        @pl.when(is_last)
        def _():
            end_swap(2, 3, 1)
            add_cross((3,), 0, stations)

    two_windows(0, 0, chunk)
    if early:
        start_swap(1, 1, 2)
    finish_early_windows()

    @pl.loop(1, CHUNKS - 1)
    def _(c):
        two_windows(c, c * chunk, chunk)

    last_half = stations - half
    two_windows(CHUNKS - 1, last_half - half, half)
    if early:
        end_swap(1, 1, 2)
        add_cross((1, 2), 0, last_half)
    two_windows(CHUNKS, last_half, half)
    if not early:
        start_swap(1, 1, 2)
        end_swap(1, 1, 2)
    copies[2].wait()
    pending = last_half if early else 0

    span = pairs // PIECES

    def share(c, piece):
        return lax.dot_general(
            lags[pl.ds(pl.multiple_of(c * lag_rows, lag_rows), lag_rows)],
            cross[pl.ds(pl.multiple_of(piece * span, span), span)],
            (((1,), (1,)), ((), ())),
            preferred_element_type=jnp.float32,
        )

    def up(index):
        return pltpu.make_async_remote_copy(
            src_ref=up_send.at[index],
            dst_ref=up_recv.at[index],
            send_sem=up_send_sem.at[index],
            recv_sem=up_recv_sem.at[index],
            device_id={"tm": tm + 1},
            device_id_type=MESH,
        )

    def down(index):
        return pltpu.make_async_remote_copy(
            src_ref=down_send.at[index],
            dst_ref=down_recv.at[index],
            send_sem=down_send_sem.at[index],
            recv_sem=down_recv_sem.at[index],
            device_id={"tm": tm - 1},
            device_id_type=MESH,
        )

    @pl.loop(0, (n_tm - 1) * PIECES)
    def _(t):
        @pl.when(t < PIECES)
        def _():
            cross_part(t, (1, 2), pending, stations, final=True)

        up_item = t - tm
        up_chunk = n_tm - 1 - up_item // PIECES
        up_piece = up_item % PIECES

        @pl.when((up_item >= 0) & (up_item < (n_tm - 1 - tm) * PIECES))
        def _():
            index = up_chunk * PIECES + up_piece
            own_share = share(up_chunk, up_piece)

            @pl.when(has_prev)
            def _():
                up(index).wait_recv()
                up_send[index] = (own_share + up_recv[index].astype(jnp.float32)).astype(
                    jnp.bfloat16
                )

            @pl.when(tm == 0)
            def _():
                up_send[index] = own_share.astype(jnp.bfloat16)

            up(index).start()

        down_item = t - (n_tm - 1 - tm)
        down_chunk = down_item // PIECES
        down_piece = down_item % PIECES

        @pl.when((down_item >= 0) & (down_item < tm * PIECES))
        def _():
            index = down_chunk * PIECES + down_piece
            own_share = share(down_chunk, down_piece)

            @pl.when(has_next)
            def _():
                down(index).wait_recv()
                down_send[index] = (own_share + down_recv[index].astype(jnp.float32)).astype(
                    jnp.bfloat16
                )

            @pl.when(is_last)
            def _():
                down_send[index] = own_share.astype(jnp.bfloat16)

            down(index).start()

    scaling = 1.0 / math.sqrt(NF * 3 * n_tm)
    for piece in range(PIECES):
        index = tm * PIECES + piece
        columns = slice(piece * span, (piece + 1) * span)
        out[:, columns] = share(tm, piece) * scaling

    for piece in range(PIECES):
        index = tm * PIECES + piece
        columns = slice(piece * span, (piece + 1) * span)

        @pl.when(has_prev)
        def _():
            up(index).wait_recv()
            out[:, columns] += up_recv[index].astype(jnp.float32) * scaling

        @pl.when(has_next)
        def _():
            down(index).wait_recv()
            out[:, columns] += down_recv[index].astype(jnp.float32) * scaling

    @pl.when(has_next)
    def _():
        offset_up.wait_send()

    for c in range(CHUNKS + 1):

        @pl.when(has_next)
        def _():
            rim_up(c).wait_send()

        @pl.when(has_prev)
        def _():
            rim_down(c).wait_send()

    @pl.loop(0, n_tm * PIECES)
    def _(index):
        @pl.when(index >= (tm + 1) * PIECES)
        def _():
            up(index).wait_send()

        @pl.when(index < tm * PIECES)
        def _():
            down(index).wait_send()


def on_device(n_tm, n_sta, traces, offsets, pair_first, pair_slot, send_rows):
    stations = traces.shape[0]
    pairs = pair_first.shape[0]
    slots = n_sta * CAP
    lag_rows = NL // n_tm
    chunk = stations // CHUNKS
    items = n_tm * PIECES
    bf16, f32 = jnp.bfloat16, jnp.float32
    vmem = pl.BlockSpec(memory_space=pltpu.VMEM)
    smem = pl.BlockSpec(memory_space=pltpu.SMEM)
    hbm = pl.BlockSpec(memory_space=pl.ANY)
    dma = pltpu.SemaphoreType.DMA
    strip = pltpu.VMEM((items, lag_rows, pairs // PIECES), bf16)
    return pl.pallas_call(
        functools.partial(kernel, n_tm, n_sta),
        out_shape=jax.ShapeDtypeStruct((lag_rows, pairs), f32),
        in_specs=[smem, vmem, vmem, vmem, vmem, hbm, hbm, hbm],
        out_specs=vmem,
        scratch_shapes=[
            pltpu.VMEM((stations, TB), bf16),
            pltpu.VMEM((stations, TB), bf16),
            pltpu.VMEM((stations, STEP), bf16),
            pltpu.VMEM((stations, STEP), bf16),
            pltpu.VMEM((WIN, 2 * NF), bf16),
            pltpu.VMEM((NL, 2 * NF), bf16),
            pltpu.VMEM((stations, WIN), bf16),
            pltpu.VMEM((stations, 2 * NF), f32),
            pltpu.VMEM((4, stations, 2 * NF), bf16),
            pltpu.VMEM((4, slots, 2 * NF), bf16),
            pltpu.VMEM((4, slots, 2 * NF), bf16),
            pltpu.VMEM((pairs, stations), bf16),
            pltpu.VMEM((pairs, slots), bf16),
            pltpu.VMEM((slots, stations), bf16),
            pltpu.VMEM((stations, stations), bf16),
            pltpu.VMEM((pairs, stations), bf16),
            pltpu.VMEM((slots, stations), bf16),
            pltpu.VMEM((4, pairs, 2 * NF), bf16),
            pltpu.VMEM((pairs, 2 * NF), f32),
            pltpu.VMEM((pairs, 2 * NF), bf16),
            strip,
            strip,
            strip,
            strip,
            pltpu.VMEM((8, BLK), jnp.int32),
            pltpu.VMEM((8, BLK), jnp.int32),
            dma((3,)),
            dma((2, CHUNKS + 1)),
            dma((2, CHUNKS + 1)),
            dma((2,)),
            dma((3, n_sta)),
            dma((3, n_sta)),
            dma((items,)),
            dma((items,)),
            dma((items,)),
            dma((items,)),
        ],
        compiler_params=pltpu.CompilerParams(
            collective_id=0, has_side_effects=True, vmem_limit_bytes=56 * 1024 * 1024
        ),
    )(
        offsets,
        pair_first.reshape(1, pairs),
        pair_slot.reshape(1, pairs),
        send_rows,
        jnp.asarray(taper_table()),
        traces,
        jnp.asarray(dft_table()),
        jnp.asarray(lag_table()),
    )


def solution(mesh):
    in_specs = (P("sta", ("day", "tm")), P(("day", "tm")), P("sta"), P("sta"), P("sta", None))
    out_specs = P(("day", "tm"), "sta")
    return jax.shard_map(
        functools.partial(on_device, mesh.shape["tm"], mesh.shape["sta"]),
        mesh=mesh,
        in_specs=in_specs,
        out_specs=out_specs,
        check_vma=False,
    )
```

```python
import functools
import math

import jax
import jax.numpy as jnp
import numpy as np
from jax import lax
from jax.experimental import pallas as pl
from jax.experimental.pallas import tpu as pltpu
from jax.sharding import PartitionSpec as P

WIN = 2048
NF = 512
NL = 1024
STEP = 1024
TB = 3072
CAP = 32
FAR_ROWS = 16
FLOOR = 0.1
CHUNKS = 4
PIECES = 4
BLK = 128
ROWS = 16
MESH = pl.DeviceIdType.MESH


def taper_table():
    n = np.arange(WIN, dtype=np.float64)
    return (0.5 - 0.5 * np.cos(2.0 * np.pi * n / WIN)).astype(np.float32)[None, :]


def dft_table():
    n = np.arange(WIN)[:, None]
    k = np.arange(NF)[None, :] + 1
    angle = (n * k % WIN) * (2.0 * np.pi / WIN)
    return np.concatenate([np.cos(angle), -np.sin(angle)], axis=1).astype(jnp.bfloat16)


def lag_table():
    t = np.arange(NL)[:, None] - NL // 2
    k = np.arange(NF)[None, :] + 1
    angle = (t * k % WIN) * (2.0 * np.pi / WIN)
    return np.concatenate([np.cos(angle), -np.sin(angle)], axis=1).astype(jnp.bfloat16)


def shifted(blocks, jitter):
    wanted = len(blocks) - 8
    quotient = jitter // BLK
    rest = jitter % BLK
    for bit, count in ((8, wanted + 8), (4, wanted + 4), (2, wanted + 2), (1, wanted + 1)):
        on = (quotient // bit) % 2 == 1
        blocks = [
            jnp.where(on, blocks[i + bit], blocks[i]) if i + bit < len(blocks) else blocks[i]
            for i in range(count)
        ]
    turn = (BLK - rest) % BLK
    rolled = [pltpu.roll(b, turn, 1) for b in blocks]
    lane = lax.broadcasted_iota(jnp.int32, blocks[0].shape, 1)
    keep = lane < BLK - rest
    return [jnp.where(keep, rolled[i], rolled[i + 1]) for i in range(wanted)]


def write_segment(blocks, jitter, taper, seg, row, means=None):
    values = [v.astype(jnp.float32) for v in shifted(blocks, jitter)]
    sums = values
    while len(sums) > 1:
        sums = [a + b for a, b in zip(sums[::2], sums[1::2])]
    total = sums[0]
    mean = jnp.sum(total, axis=1, keepdims=True) * (1.0 / WIN)
    if means is not None:
        means[pl.ds(row, ROWS)] = jnp.broadcast_to(mean, (ROWS, BLK))
    for i, v in enumerate(values):
        columns = slice(i * BLK, (i + 1) * BLK)
        seg[pl.ds(row, ROWS), columns] = ((v - mean) * taper[:, columns]).astype(jnp.bfloat16)


def taper_rest():
    rest = taper_table()[0, STEP:].astype(np.float64) @ dft_table()[STEP:].astype(np.float64)
    return rest.astype(np.float32)[None, :]


def load_blocks(ref, row, first, count):
    return [
        ref[pl.ds(row, ROWS), i * BLK : (i + 1) * BLK]
        for i in range(first, first + count)
    ]


def whiten_rows(spec, row):
    re = spec[pl.ds(row, ROWS), :NF]
    im = spec[pl.ds(row, ROWS), NF:]
    amplitude = jnp.sqrt(re * re + im * im + 1e-06)
    wide = jnp.concatenate([amplitude, jnp.zeros((ROWS, BLK), jnp.float32)], axis=1)
    width = NF + BLK
    pair = wide + pltpu.roll(wide, 1, 1)
    five = wide + pltpu.roll(pair, 1, 1) + pltpu.roll(pair, width - 2, 1)
    inverse = 1.0 / jnp.maximum(five[:, :NF] * (1.0 / 5.0), FLOOR)
    return (re * inverse).astype(jnp.bfloat16), (im * inverse).astype(jnp.bfloat16)


def kernel(
    n_tm, n_sta,
    offsets, pair_first, pair_slot, send_rows, taper, rest, traces, table_hbm, lag_hbm,
    out,
    raw, own, rim_prev, rim_next, table, lags, seg, spec, means, white, outgoing, incoming,
    pick_first, pick_second, pick_send, order, first_at, send_at, second_rows, cross_sum, cross,
    up_send, up_recv, down_send, down_recv, offset_send, offset_recv,
    local_sem, rim_send_sem, rim_recv_sem, offset_sem, swap_send_sem, swap_recv_sem,
    up_send_sem, up_recv_sem, down_send_sem, down_recv_sem,
):
    stations = own.shape[0]
    pairs = out.shape[1]
    lag_rows = out.shape[0]
    slots = n_sta * CAP
    chunk = stations // CHUNKS
    half = chunk // 2
    early = slots <= chunk
    tm = lax.axis_index("tm")
    me = lax.axis_index("sta")
    has_prev = tm > 0
    has_next = tm < n_tm - 1
    is_last = tm == n_tm - 1

    def load_columns(first, last, index):
        columns = pl.ds(first, last - first)
        return pltpu.make_async_copy(
            traces.at[:, columns], raw.at[:, columns], local_sem.at[index]
        )

    load_head = load_columns(0, STEP, 0)
    load_tail = load_columns(TB - STEP, TB, 1)
    load_middle = load_columns(STEP, TB - STEP, 2)
    load_table = pltpu.make_async_copy(table_hbm, table, local_sem.at[3])
    load_lags = pltpu.make_async_copy(lag_hbm, lags, local_sem.at[4])
    load_head.start()
    load_tail.start()

    incoming[...] = jnp.zeros_like(incoming)
    offset_send[...] = jnp.full(offset_send.shape, offsets[2], jnp.int32)

    @pl.when(tm == 0)
    def _():
        rim_prev[...] = jnp.zeros_like(rim_prev)
        offset_recv[...] = jnp.full(offset_recv.shape, 2 * STEP, jnp.int32)

    @pl.when(is_last)
    def _():
        rim_next[...] = jnp.zeros_like(rim_next)

    barrier = pltpu.get_barrier_semaphore()
    for delta in range(1, n_sta):
        pl.semaphore_signal(
            barrier, inc=1, device_id={"sta": (me + delta) % n_sta}, device_id_type=MESH
        )

    @pl.when(has_prev)
    def _():
        pl.semaphore_signal(barrier, inc=1, device_id={"tm": tm - 1}, device_id_type=MESH)

    @pl.when(has_next)
    def _():
        pl.semaphore_signal(barrier, inc=1, device_id={"tm": tm + 1}, device_id_type=MESH)

    def rim_rows(c):
        if isinstance(c, int) and c >= CHUNKS - 1:
            return pl.ds((CHUNKS - 1) * chunk + (c - CHUNKS + 1) * half, half)
        return pl.ds(c * chunk, chunk)

    def rim_up(c):
        rows = rim_rows(c)
        return pltpu.make_async_remote_copy(
            src_ref=own.at[rows, pl.ds(TB - STEP, STEP)],
            dst_ref=rim_prev.at[rows],
            send_sem=rim_send_sem.at[0, c],
            recv_sem=rim_recv_sem.at[0, c],
            device_id={"tm": tm + 1},
            device_id_type=MESH,
        )

    def rim_down(c):
        rows = rim_rows(c)
        return pltpu.make_async_remote_copy(
            src_ref=own.at[rows, pl.ds(0, STEP)],
            dst_ref=rim_next.at[rows],
            send_sem=rim_send_sem.at[1, c],
            recv_sem=rim_recv_sem.at[1, c],
            device_id={"tm": tm - 1},
            device_id_type=MESH,
        )

    offset_up = pltpu.make_async_remote_copy(
        src_ref=offset_send,
        dst_ref=offset_recv,
        send_sem=offset_sem.at[0],
        recv_sem=offset_sem.at[1],
        device_id={"tm": tm + 1},
        device_id_type=MESH,
    )

    def one_hot(ref, values, depth):
        count = values.shape[1]
        spread = jnp.transpose(jnp.broadcast_to(values.astype(jnp.float32), (BLK, count)))
        lane = lax.broadcasted_iota(jnp.int32, (count, BLK), 1).astype(jnp.float32)
        for b in range(depth // BLK):
            ref[:, b * BLK : (b + 1) * BLK] = (
                (spread == lane + float(b * BLK)).astype(jnp.float32).astype(jnp.bfloat16)
            )

    one_hot(pick_send, send_rows[...], stations)
    hits = jnp.dot(
        jnp.ones((8, slots), jnp.bfloat16), pick_send[...], preferred_element_type=jnp.float32
    )
    chosen = hits > 0.5
    mark = chosen.astype(jnp.float32)
    from_row = lax.broadcasted_iota(jnp.int32, (stations, stations), 0)
    to_lane = lax.broadcasted_iota(jnp.int32, (stations, stations), 1)
    up_to = (from_row <= to_lane).astype(jnp.float32).astype(jnp.bfloat16)
    running = jnp.dot(mark.astype(jnp.bfloat16), up_to, preferred_element_type=jnp.float32)
    lane = lax.broadcasted_iota(jnp.int32, (8, stations), 1).astype(jnp.float32)
    total = jnp.sum(mark, axis=1, keepdims=True)
    place = jnp.where(chosen, running - 1.0, total + lane - running)
    order[...] = (
        (place[:1] == from_row.astype(jnp.float32)).astype(jnp.float32).astype(jnp.bfloat16)
    )

    load_head.wait()
    load_tail.wait()
    load_middle.start()
    load_table.start()
    load_lags.start()

    def arrange(rows, columns):
        own[rows, columns] = jnp.dot(
            order[rows], raw[:, columns], preferred_element_type=jnp.float32
        ).astype(jnp.bfloat16)

    for c in range(CHUNKS + 1):
        arrange(rim_rows(c), slice(0, STEP))
        arrange(rim_rows(c), slice(TB - STEP, TB))

        if c == 0:
            greeted = n_sta - 1 + has_prev.astype(jnp.int32) + has_next.astype(jnp.int32)
            pl.semaphore_wait(barrier, greeted)

            @pl.when(has_next)
            def _():
                offset_up.start()

        @pl.when(has_next)
        def _():
            rim_up(c).start()

        @pl.when(has_prev)
        def _():
            rim_down(c).start()

    load_middle.wait()
    arrange(slice(0, stations), slice(STEP, TB - STEP))

    def in_order(ref):
        return lax.dot_general(
            ref[...], order[...], (((1,), (1,)), ((), ())),
            preferred_element_type=jnp.float32,
        ).astype(jnp.bfloat16)

    one_hot(pick_first, pair_first[...], stations)
    one_hot(pick_second, pair_slot[...], slots)
    first_at[...] = in_order(pick_first)
    send_at[...] = in_order(pick_send)
    load_table.wait()

    scale = 1.0 / math.sqrt(WIN)

    def transform(count):
        spec[:count] = (
            jnp.dot(seg[:count], table[...], preferred_element_type=jnp.float32) * scale
        )

    def transform_half():
        first = jnp.dot(
            seg[:, :STEP], table[:STEP], preferred_element_type=jnp.float32
        )
        spec[...] = (first - means[:, :1] * rest[...]) * scale

    def single_window(slot, jitter, blocks_at, half_window=False):
        @pl.loop(0, stations // ROWS, unroll=4)
        def _(g):
            row = pl.multiple_of(g * ROWS, ROWS)
            write_segment(
                blocks_at(row), jitter, taper, seg, row, means if half_window else None
            )

        if half_window:
            transform_half()
        else:
            transform(stations)

        @pl.loop(0, stations // ROWS, unroll=4)
        def _(g):
            row = pl.multiple_of(g * ROWS, ROWS)
            re, im = whiten_rows(spec, row)
            white[slot, pl.ds(row, ROWS), :NF] = re
            white[slot, pl.ds(row, ROWS), NF:] = im

    def swap(which, slot, depth):
        result = []
        for delta in range(1, n_sta):
            rows = CAP if min(delta, n_sta - delta) <= 1 else FAR_ROWS
            partner = (me + delta) % n_sta
            result.append(
                pltpu.make_async_remote_copy(
                    src_ref=outgoing.at[
                        pl.ds(slot, depth), pl.ds(pl.multiple_of(partner * CAP, CAP), rows)
                    ],
                    dst_ref=incoming.at[
                        pl.ds(slot, depth), pl.ds(pl.multiple_of(me * CAP, CAP), rows)
                    ],
                    send_sem=swap_send_sem.at[which, delta],
                    recv_sem=swap_recv_sem.at[which, delta],
                    device_id={"sta": partner},
                    device_id_type=MESH,
                )
            )
        return result

    lead = min(slots, stations)

    def start_swap(which, slot, depth):
        for w in range(slot, slot + depth):
            outgoing[w] = jnp.dot(
                send_at[:, :lead], white[w, :lead], preferred_element_type=jnp.float32
            ).astype(jnp.bfloat16)
        for copy in swap(which, slot, depth):
            copy.start()
        mine = pl.ds(pl.multiple_of(me * CAP, CAP), CAP)
        for w in range(slot, slot + depth):
            incoming[w, mine] = outgoing[w, mine]

    def end_swap(which, slot, depth):
        for copy in swap(which, slot, depth):
            copy.wait()
        for w in range(slot, slot + depth):
            second_rows[w] = jnp.dot(
                pick_second[...], incoming[w], preferred_element_type=jnp.float32
            ).astype(jnp.bfloat16)

    part = pairs // PIECES
    width = 256

    def cross_part(p, windows, low, high, fresh=False, final=False):
        rows = pl.ds(pl.multiple_of(p * part, part), part)
        for b in range(NF // width):
            rcol = slice(b * width, (b + 1) * width)
            icol = slice(NF + b * width, NF + (b + 1) * width)
            real = None if fresh else cross_sum[rows, rcol]
            imag = None if fresh else cross_sum[rows, icol]
            for w in windows:
                fr, fi = [
                    jnp.dot(
                        first_at[rows, low:high], white[w, low:high, columns],
                        preferred_element_type=jnp.float32,
                    )
                    for columns in (rcol, icol)
                ]
                sr = second_rows[w, rows, rcol].astype(jnp.float32)
                si = second_rows[w, rows, icol].astype(jnp.float32)
                new_real = fr * sr + fi * si
                new_imag = fi * sr - fr * si
                real = new_real if real is None else real + new_real
                imag = new_imag if imag is None else imag + new_imag
            if final:
                cross[rows, rcol] = real.astype(jnp.bfloat16)
                cross[rows, icol] = imag.astype(jnp.bfloat16)
            else:
                cross_sum[rows, rcol] = real
                cross_sum[rows, icol] = imag

    def add_cross(windows, low, high, fresh=False):
        @pl.loop(0, PIECES)
        def _(p):
            cross_part(p, windows, low, high, fresh=fresh)

    single_window(0, offsets[0], lambda row: load_blocks(own, row, 0, 24))
    start_swap(0, 0, 1)

    @pl.when(is_last)
    def _():
        single_window(
            3,
            offsets[2] - 2 * STEP,
            lambda row: load_blocks(own, row, 16, 8)
            + [jnp.zeros((ROWS, BLK), jnp.bfloat16)] * 8,
            half_window=True,
        )
        start_swap(2, 3, 1)

    @pl.when(has_prev)
    def _():
        offset_up.wait_recv()

    jitter_1 = offsets[1] - STEP
    jitter_2 = offset_recv[0, 0] - 2 * STEP
    keep = jnp.where(has_prev, 1.0, 0.0).astype(jnp.float32)

    def two_windows(c, start, size):
        @pl.when(has_prev)
        def _():
            rim_up(c).wait_recv()

        @pl.when(has_next)
        def _():
            rim_down(c).wait_recv()

        @pl.loop(0, size // ROWS, unroll=2)
        def _(g):
            row = pl.multiple_of(start + g * ROWS, ROWS)
            at = pl.multiple_of(g * ROWS, ROWS)
            write_segment(
                load_blocks(own, row, 8, 16) + load_blocks(rim_next, row, 0, 8),
                jitter_1, taper, seg, at,
            )
            write_segment(
                load_blocks(rim_prev, row, 0, 8) + load_blocks(own, row, 0, 16),
                jitter_2, taper, seg, pl.multiple_of(size + g * ROWS, ROWS),
            )

        transform(2 * size)

        @pl.loop(0, size // ROWS, unroll=2)
        def _(g):
            row = pl.multiple_of(start + g * ROWS, ROWS)
            re, im = whiten_rows(spec, pl.multiple_of(g * ROWS, ROWS))
            white[1, pl.ds(row, ROWS), :NF] = re
            white[1, pl.ds(row, ROWS), NF:] = im
            re, im = whiten_rows(spec, pl.multiple_of(size + g * ROWS, ROWS))
            white[2, pl.ds(row, ROWS), :NF] = (re * keep).astype(jnp.bfloat16)
            white[2, pl.ds(row, ROWS), NF:] = (im * keep).astype(jnp.bfloat16)

    def finish_early_windows():
        end_swap(0, 0, 1)
        add_cross((0,), 0, stations, fresh=True)

        @pl.when(is_last)
        def _():
            end_swap(2, 3, 1)
            add_cross((3,), 0, stations)

    two_windows(0, 0, chunk)
    if early:
        start_swap(1, 1, 2)
    finish_early_windows()

    @pl.loop(1, CHUNKS - 1)
    def _(c):
        two_windows(c, c * chunk, chunk)

    last = stations - chunk
    if early:
        end_swap(1, 1, 2)
        add_cross((1, 2), 0, last)
    two_windows(CHUNKS - 1, last, half)
    two_windows(CHUNKS, last + half, half)
    if not early:
        start_swap(1, 1, 2)
        end_swap(1, 1, 2)
    load_lags.wait()
    pending = last if early else 0

    span = pairs // PIECES

    def share(c, piece):
        return lax.dot_general(
            lags[pl.ds(pl.multiple_of(c * lag_rows, lag_rows), lag_rows)],
            cross[pl.ds(pl.multiple_of(piece * span, span), span)],
            (((1,), (1,)), ((), ())),
            preferred_element_type=jnp.float32,
        )

    def up(index):
        return pltpu.make_async_remote_copy(
            src_ref=up_send.at[index],
            dst_ref=up_recv.at[index],
            send_sem=up_send_sem.at[index],
            recv_sem=up_recv_sem.at[index],
            device_id={"tm": tm + 1},
            device_id_type=MESH,
        )

    def down(index):
        return pltpu.make_async_remote_copy(
            src_ref=down_send.at[index],
            dst_ref=down_recv.at[index],
            send_sem=down_send_sem.at[index],
            recv_sem=down_recv_sem.at[index],
            device_id={"tm": tm - 1},
            device_id_type=MESH,
        )

    @pl.loop(0, (n_tm - 1) * PIECES)
    def _(t):
        @pl.when(t < PIECES)
        def _():
            cross_part(t, (1, 2), pending, stations, final=True)

        up_item = t - tm
        up_chunk = n_tm - 1 - up_item // PIECES
        up_piece = up_item % PIECES

        @pl.when((up_item >= 0) & (up_item < (n_tm - 1 - tm) * PIECES))
        def _():
            index = up_chunk * PIECES + up_piece
            own_share = share(up_chunk, up_piece)

            @pl.when(has_prev)
            def _():
                up(index).wait_recv()
                up_send[index] = (own_share + up_recv[index].astype(jnp.float32)).astype(
                    jnp.bfloat16
                )

            @pl.when(tm == 0)
            def _():
                up_send[index] = own_share.astype(jnp.bfloat16)

            up(index).start()

        down_item = t - (n_tm - 1 - tm)
        down_chunk = down_item // PIECES
        down_piece = down_item % PIECES

        @pl.when((down_item >= 0) & (down_item < tm * PIECES))
        def _():
            index = down_chunk * PIECES + down_piece
            own_share = share(down_chunk, down_piece)

            @pl.when(has_next)
            def _():
                down(index).wait_recv()
                down_send[index] = (own_share + down_recv[index].astype(jnp.float32)).astype(
                    jnp.bfloat16
                )

            @pl.when(is_last)
            def _():
                down_send[index] = own_share.astype(jnp.bfloat16)

            down(index).start()

    scaling = 1.0 / math.sqrt(NF * 3 * n_tm)
    for piece in range(PIECES):
        index = tm * PIECES + piece
        columns = slice(piece * span, (piece + 1) * span)
        out[:, columns] = share(tm, piece) * scaling

    for piece in range(PIECES):
        index = tm * PIECES + piece
        columns = slice(piece * span, (piece + 1) * span)

        @pl.when(has_prev)
        def _():
            up(index).wait_recv()
            out[:, columns] += up_recv[index].astype(jnp.float32) * scaling

        @pl.when(has_next)
        def _():
            down(index).wait_recv()
            out[:, columns] += down_recv[index].astype(jnp.float32) * scaling

    @pl.when(has_next)
    def _():
        offset_up.wait_send()

    for c in range(CHUNKS + 1):

        @pl.when(has_next)
        def _():
            rim_up(c).wait_send()

        @pl.when(has_prev)
        def _():
            rim_down(c).wait_send()

    @pl.loop(0, n_tm * PIECES)
    def _(index):
        @pl.when(index >= (tm + 1) * PIECES)
        def _():
            up(index).wait_send()

        @pl.when(index < tm * PIECES)
        def _():
            down(index).wait_send()


def on_device(n_tm, n_sta, traces, offsets, pair_first, pair_slot, send_rows):
    stations = traces.shape[0]
    pairs = pair_first.shape[0]
    slots = n_sta * CAP
    lag_rows = NL // n_tm
    chunk = stations // CHUNKS
    items = n_tm * PIECES
    bf16, f32 = jnp.bfloat16, jnp.float32
    vmem = pl.BlockSpec(memory_space=pltpu.VMEM)
    smem = pl.BlockSpec(memory_space=pltpu.SMEM)
    hbm = pl.BlockSpec(memory_space=pl.ANY)
    dma = pltpu.SemaphoreType.DMA
    strip = pltpu.VMEM((items, lag_rows, pairs // PIECES), bf16)
    return pl.pallas_call(
        functools.partial(kernel, n_tm, n_sta),
        out_shape=jax.ShapeDtypeStruct((lag_rows, pairs), f32),
        in_specs=[smem, vmem, vmem, vmem, vmem, vmem, hbm, hbm, hbm],
        out_specs=vmem,
        scratch_shapes=[
            pltpu.VMEM((stations, TB), bf16),
            pltpu.VMEM((stations, TB), bf16),
            pltpu.VMEM((stations, STEP), bf16),
            pltpu.VMEM((stations, STEP), bf16),
            pltpu.VMEM((WIN, 2 * NF), bf16),
            pltpu.VMEM((NL, 2 * NF), bf16),
            pltpu.VMEM((stations, WIN), bf16),
            pltpu.VMEM((stations, 2 * NF), f32),
            pltpu.VMEM((stations, BLK), f32),
            pltpu.VMEM((4, stations, 2 * NF), bf16),
            pltpu.VMEM((4, slots, 2 * NF), bf16),
            pltpu.VMEM((4, slots, 2 * NF), bf16),
            pltpu.VMEM((pairs, stations), bf16),
            pltpu.VMEM((pairs, slots), bf16),
            pltpu.VMEM((slots, stations), bf16),
            pltpu.VMEM((stations, stations), bf16),
            pltpu.VMEM((pairs, stations), bf16),
            pltpu.VMEM((slots, stations), bf16),
            pltpu.VMEM((4, pairs, 2 * NF), bf16),
            pltpu.VMEM((pairs, 2 * NF), f32),
            pltpu.VMEM((pairs, 2 * NF), bf16),
            strip,
            strip,
            strip,
            strip,
            pltpu.VMEM((8, BLK), jnp.int32),
            pltpu.VMEM((8, BLK), jnp.int32),
            dma((5,)),
            dma((2, CHUNKS + 1)),
            dma((2, CHUNKS + 1)),
            dma((2,)),
            dma((3, n_sta)),
            dma((3, n_sta)),
            dma((items,)),
            dma((items,)),
            dma((items,)),
            dma((items,)),
        ],
        compiler_params=pltpu.CompilerParams(
            collective_id=0, has_side_effects=True, vmem_limit_bytes=56 * 1024 * 1024
        ),
    )(
        offsets,
        pair_first.reshape(1, pairs),
        pair_slot.reshape(1, pairs),
        send_rows,
        jnp.asarray(taper_table()),
        jnp.asarray(taper_rest()),
        traces,
        jnp.asarray(dft_table()),
        jnp.asarray(lag_table()),
    )


def solution(mesh):
    in_specs = (P("sta", ("day", "tm")), P(("day", "tm")), P("sta"), P("sta"), P("sta", None))
    out_specs = P(("day", "tm"), "sta")
    return jax.shard_map(
        functools.partial(on_device, mesh.shape["tm"], mesh.shape["sta"]),
        mesh=mesh,
        in_specs=in_specs,
        out_specs=out_specs,
        check_vma=False,
    )
```

```python
import functools
import math

import jax
import jax.numpy as jnp
import numpy as np
from jax import lax
from jax.experimental import pallas as pl
from jax.experimental.pallas import tpu as pltpu
from jax.sharding import PartitionSpec as P

WIN = 2048
NF = 512
NL = 1024
STEP = 1024
TB = 3072
CAP = 32
FAR_ROWS = 16
FLOOR = 0.1
CHUNKS = 4
PIECES = 2
BLK = 128
ROWS = 16
MESH = pl.DeviceIdType.MESH


def taper_table():
    n = np.arange(WIN, dtype=np.float64)
    return (0.5 - 0.5 * np.cos(2.0 * np.pi * n / WIN)).astype(np.float32)[None, :]


def dft_table():
    n = np.arange(WIN)[:, None]
    k = np.arange(NF)[None, :] + 1
    angle = (n * k % WIN) * (2.0 * np.pi / WIN)
    return np.concatenate([np.cos(angle), -np.sin(angle)], axis=1).astype(jnp.bfloat16)


def lag_table():
    t = np.arange(NL)[:, None] - NL // 2
    k = np.arange(NF)[None, :] + 1
    angle = (t * k % WIN) * (2.0 * np.pi / WIN)
    return np.concatenate([np.cos(angle), -np.sin(angle)], axis=1).astype(jnp.bfloat16)


def shifted(blocks, jitter):
    wanted = len(blocks) - 8
    quotient = jitter // BLK
    rest = jitter % BLK
    for bit, count in ((8, wanted + 8), (4, wanted + 4), (2, wanted + 2), (1, wanted + 1)):
        on = (quotient // bit) % 2 == 1
        blocks = [
            jnp.where(on, blocks[i + bit], blocks[i]) if i + bit < len(blocks) else blocks[i]
            for i in range(count)
        ]
    turn = (BLK - rest) % BLK
    rolled = [pltpu.roll(b, turn, 1) for b in blocks]
    lane = lax.broadcasted_iota(jnp.int32, blocks[0].shape, 1)
    keep = lane < BLK - rest
    return [jnp.where(keep, rolled[i], rolled[i + 1]) for i in range(wanted)]


def write_segment(blocks, jitter, taper, seg, row, means=None):
    values = [v.astype(jnp.float32) for v in shifted(blocks, jitter)]
    sums = values
    while len(sums) > 1:
        sums = [a + b for a, b in zip(sums[::2], sums[1::2])]
    total = sums[0]
    mean = jnp.sum(total, axis=1, keepdims=True) * (1.0 / WIN)
    if means is not None:
        means[pl.ds(row, ROWS)] = jnp.broadcast_to(mean, (ROWS, BLK))
    for i, v in enumerate(values):
        columns = slice(i * BLK, (i + 1) * BLK)
        seg[pl.ds(row, ROWS), columns] = ((v - mean) * taper[:, columns]).astype(jnp.bfloat16)


def taper_rest():
    rest = taper_table()[0, STEP:].astype(np.float64) @ dft_table()[STEP:].astype(np.float64)
    return rest.astype(np.float32)[None, :]


def load_blocks(ref, row, first, count):
    return [
        ref[pl.ds(row, ROWS), i * BLK : (i + 1) * BLK]
        for i in range(first, first + count)
    ]


def whiten_rows(spec, row):
    re = spec[pl.ds(row, ROWS), :NF]
    im = spec[pl.ds(row, ROWS), NF:]
    amplitude = jnp.sqrt(re * re + im * im + 1e-06)
    wide = jnp.concatenate([amplitude, jnp.zeros((ROWS, BLK), jnp.float32)], axis=1)
    width = NF + BLK
    pair = wide + pltpu.roll(wide, 1, 1)
    five = wide + pltpu.roll(pair, 1, 1) + pltpu.roll(pair, width - 2, 1)
    inverse = 1.0 / jnp.maximum(five[:, :NF] * (1.0 / 5.0), FLOOR)
    return (re * inverse).astype(jnp.bfloat16), (im * inverse).astype(jnp.bfloat16)


def kernel(
    n_tm, n_sta,
    offsets, pair_first, pair_slot, send_rows, taper, rest, traces, table_hbm, lag_hbm,
    out,
    raw, own, rim_prev, rim_next, table, lags, seg, spec, means, white, outgoing, incoming,
    pick_first, pick_second, pick_send, order, first_at, send_at, second_rows, cross_sum, cross,
    up_send, up_recv, down_send, down_recv, offset_send, offset_recv,
    local_sem, rim_send_sem, rim_recv_sem, offset_sem, swap_send_sem, swap_recv_sem,
    up_send_sem, up_recv_sem, down_send_sem, down_recv_sem,
):
    stations = own.shape[0]
    pairs = out.shape[1]
    lag_rows = out.shape[0]
    slots = n_sta * CAP
    chunk = stations // CHUNKS
    half = chunk // 2
    early = slots <= chunk
    tm = lax.axis_index("tm")
    me = lax.axis_index("sta")
    has_prev = tm > 0
    has_next = tm < n_tm - 1
    is_last = tm == n_tm - 1

    def load_columns(first, last, index):
        columns = pl.ds(first, last - first)
        return pltpu.make_async_copy(
            traces.at[:, columns], raw.at[:, columns], local_sem.at[index]
        )

    load_head = load_columns(0, STEP, 0)
    load_tail = load_columns(TB - STEP, TB, 1)
    load_middle = load_columns(STEP, TB - STEP, 2)
    load_table = pltpu.make_async_copy(table_hbm, table, local_sem.at[3])
    load_lags = pltpu.make_async_copy(lag_hbm, lags, local_sem.at[4])
    load_head.start()
    load_tail.start()

    incoming[...] = jnp.zeros_like(incoming)
    offset_send[...] = jnp.full(offset_send.shape, offsets[2], jnp.int32)

    @pl.when(tm == 0)
    def _():
        rim_prev[...] = jnp.zeros_like(rim_prev)
        offset_recv[...] = jnp.full(offset_recv.shape, 2 * STEP, jnp.int32)

    @pl.when(is_last)
    def _():
        rim_next[...] = jnp.zeros_like(rim_next)

    barrier = pltpu.get_barrier_semaphore()
    for delta in range(1, n_sta):
        pl.semaphore_signal(
            barrier, inc=1, device_id={"sta": (me + delta) % n_sta}, device_id_type=MESH
        )

    @pl.when(has_prev)
    def _():
        pl.semaphore_signal(barrier, inc=1, device_id={"tm": tm - 1}, device_id_type=MESH)

    @pl.when(has_next)
    def _():
        pl.semaphore_signal(barrier, inc=1, device_id={"tm": tm + 1}, device_id_type=MESH)

    def rim_rows(c):
        if isinstance(c, int) and c >= CHUNKS - 1:
            return pl.ds((CHUNKS - 1) * chunk + (c - CHUNKS + 1) * half, half)
        return pl.ds(c * chunk, chunk)

    def source(c):
        return traces if isinstance(c, int) and c == 0 else own

    def rim_up(c):
        rows = rim_rows(c)
        return pltpu.make_async_remote_copy(
            src_ref=source(c).at[rows, pl.ds(TB - STEP, STEP)],
            dst_ref=rim_prev.at[rows],
            send_sem=rim_send_sem.at[0, c],
            recv_sem=rim_recv_sem.at[0, c],
            device_id={"tm": tm + 1},
            device_id_type=MESH,
        )

    def rim_down(c):
        rows = rim_rows(c)
        return pltpu.make_async_remote_copy(
            src_ref=source(c).at[rows, pl.ds(0, STEP)],
            dst_ref=rim_next.at[rows],
            send_sem=rim_send_sem.at[1, c],
            recv_sem=rim_recv_sem.at[1, c],
            device_id={"tm": tm - 1},
            device_id_type=MESH,
        )

    offset_up = pltpu.make_async_remote_copy(
        src_ref=offset_send,
        dst_ref=offset_recv,
        send_sem=offset_sem.at[0],
        recv_sem=offset_sem.at[1],
        device_id={"tm": tm + 1},
        device_id_type=MESH,
    )

    greeted = n_sta - 1 + has_prev.astype(jnp.int32) + has_next.astype(jnp.int32)
    pl.semaphore_wait(barrier, greeted)

    @pl.when(has_next)
    def _():
        rim_up(0).start()
        offset_up.start()

    @pl.when(has_prev)
    def _():
        rim_down(0).start()

    def one_hot(ref, values, depth):
        count = values.shape[1]
        spread = jnp.transpose(jnp.broadcast_to(values.astype(jnp.float32), (BLK, count)))
        lane = lax.broadcasted_iota(jnp.int32, (count, BLK), 1).astype(jnp.float32)
        for b in range(depth // BLK):
            ref[:, b * BLK : (b + 1) * BLK] = (
                (spread == lane + float(b * BLK)).astype(jnp.float32).astype(jnp.bfloat16)
            )

    one_hot(pick_send, send_rows[...], stations)
    hits = jnp.dot(
        jnp.ones((8, slots), jnp.bfloat16), pick_send[...], preferred_element_type=jnp.float32
    )
    lane = lax.broadcasted_iota(jnp.int32, (8, stations), 1).astype(jnp.float32)
    chosen = (hits > 0.5) & (lane >= float(chunk))
    mark = chosen.astype(jnp.float32)
    from_row = lax.broadcasted_iota(jnp.int32, (stations, stations), 0)
    to_lane = lax.broadcasted_iota(jnp.int32, (stations, stations), 1)
    up_to = (from_row <= to_lane).astype(jnp.float32).astype(jnp.bfloat16)
    running = jnp.dot(mark.astype(jnp.bfloat16), up_to, preferred_element_type=jnp.float32)
    total = jnp.sum(mark, axis=1, keepdims=True)
    place = jnp.where(chosen, float(chunk - 1) + running, total + lane - running)
    place = jnp.where(lane < float(chunk), lane, place)
    order[...] = (
        (place[:1] == from_row.astype(jnp.float32)).astype(jnp.float32).astype(jnp.bfloat16)
    )

    load_head.wait()
    load_tail.wait()
    load_middle.start()
    load_table.start()
    load_lags.start()

    def arrange(rows, columns):
        own[rows, columns] = jnp.dot(
            order[rows], raw[:, columns], preferred_element_type=jnp.float32
        ).astype(jnp.bfloat16)

    for c in [*range(1, CHUNKS + 1), 0]:
        arrange(rim_rows(c), slice(0, STEP))
        arrange(rim_rows(c), slice(TB - STEP, TB))

        if c > 0:

            @pl.when(has_next)
            def _():
                rim_up(c).start()

            @pl.when(has_prev)
            def _():
                rim_down(c).start()

    load_middle.wait()
    arrange(slice(0, stations), slice(STEP, TB - STEP))

    def in_order(ref):
        return lax.dot_general(
            ref[...], order[...], (((1,), (1,)), ((), ())),
            preferred_element_type=jnp.float32,
        ).astype(jnp.bfloat16)

    one_hot(pick_first, pair_first[...], stations)
    one_hot(pick_second, pair_slot[...], slots)
    first_at[...] = in_order(pick_first)
    send_at[...] = in_order(pick_send)
    load_table.wait()

    scale = 1.0 / math.sqrt(WIN)

    def transform(count):
        spec[:count] = (
            jnp.dot(seg[:count], table[...], preferred_element_type=jnp.float32) * scale
        )

    def transform_half():
        first = jnp.dot(
            seg[:, :STEP], table[:STEP], preferred_element_type=jnp.float32
        )
        spec[...] = (first - means[:, :1] * rest[...]) * scale

    def single_window(slot, jitter, blocks_at, half_window=False):
        @pl.loop(0, stations // ROWS, unroll=4)
        def _(g):
            row = pl.multiple_of(g * ROWS, ROWS)
            write_segment(
                blocks_at(row), jitter, taper, seg, row, means if half_window else None
            )

        if half_window:
            transform_half()
        else:
            transform(stations)

        @pl.loop(0, stations // ROWS, unroll=4)
        def _(g):
            row = pl.multiple_of(g * ROWS, ROWS)
            re, im = whiten_rows(spec, row)
            white[slot, pl.ds(row, ROWS), :NF] = re
            white[slot, pl.ds(row, ROWS), NF:] = im

    def swap(which, slot, depth):
        result = []
        for delta in range(1, n_sta):
            rows = CAP if min(delta, n_sta - delta) <= 1 else FAR_ROWS
            partner = (me + delta) % n_sta
            result.append(
                pltpu.make_async_remote_copy(
                    src_ref=outgoing.at[
                        pl.ds(slot, depth), pl.ds(pl.multiple_of(partner * CAP, CAP), rows)
                    ],
                    dst_ref=incoming.at[
                        pl.ds(slot, depth), pl.ds(pl.multiple_of(me * CAP, CAP), rows)
                    ],
                    send_sem=swap_send_sem.at[which, delta],
                    recv_sem=swap_recv_sem.at[which, delta],
                    device_id={"sta": partner},
                    device_id_type=MESH,
                )
            )
        return result

    lead = 2 * chunk if early else stations

    def start_swap(which, slot, depth):
        for w in range(slot, slot + depth):
            outgoing[w] = jnp.dot(
                send_at[:, :lead], white[w, :lead], preferred_element_type=jnp.float32
            ).astype(jnp.bfloat16)
        for copy in swap(which, slot, depth):
            copy.start()
        mine = pl.ds(pl.multiple_of(me * CAP, CAP), CAP)
        for w in range(slot, slot + depth):
            incoming[w, mine] = outgoing[w, mine]

    def end_swap(which, slot, depth):
        for copy in swap(which, slot, depth):
            copy.wait()
        for w in range(slot, slot + depth):
            second_rows[w] = jnp.dot(
                pick_second[...], incoming[w], preferred_element_type=jnp.float32
            ).astype(jnp.bfloat16)

    part = pairs // PIECES
    width = 256

    def cross_part(p, windows, low, high, fresh=False, final=False):
        rows = pl.ds(pl.multiple_of(p * part, part), part)
        for b in range(NF // width):
            rcol = slice(b * width, (b + 1) * width)
            icol = slice(NF + b * width, NF + (b + 1) * width)
            real = None if fresh else cross_sum[rows, rcol]
            imag = None if fresh else cross_sum[rows, icol]
            for w in windows:
                fr, fi = [
                    jnp.dot(
                        first_at[rows, low:high], white[w, low:high, columns],
                        preferred_element_type=jnp.float32,
                    )
                    for columns in (rcol, icol)
                ]
                sr = second_rows[w, rows, rcol].astype(jnp.float32)
                si = second_rows[w, rows, icol].astype(jnp.float32)
                new_real = fr * sr + fi * si
                new_imag = fi * sr - fr * si
                real = new_real if real is None else real + new_real
                imag = new_imag if imag is None else imag + new_imag
            if final:
                cross[rows, rcol] = real.astype(jnp.bfloat16)
                cross[rows, icol] = imag.astype(jnp.bfloat16)
            else:
                cross_sum[rows, rcol] = real
                cross_sum[rows, icol] = imag

    def add_cross(windows, low, high, fresh=False):
        @pl.loop(0, PIECES)
        def _(p):
            cross_part(p, windows, low, high, fresh=fresh)

    single_window(0, offsets[0], lambda row: load_blocks(own, row, 0, 24))
    start_swap(0, 0, 1)

    @pl.when(is_last)
    def _():
        single_window(
            3,
            offsets[2] - 2 * STEP,
            lambda row: load_blocks(own, row, 16, 8)
            + [jnp.zeros((ROWS, BLK), jnp.bfloat16)] * 8,
            half_window=True,
        )
        start_swap(2, 3, 1)

    @pl.when(has_prev)
    def _():
        offset_up.wait_recv()

    jitter_1 = offsets[1] - STEP
    jitter_2 = offset_recv[0, 0] - 2 * STEP
    keep = jnp.where(has_prev, 1.0, 0.0).astype(jnp.float32)

    def two_windows(c, start, size):
        @pl.when(has_prev)
        def _():
            rim_up(c).wait_recv()

        @pl.when(has_next)
        def _():
            rim_down(c).wait_recv()

        @pl.loop(0, size // ROWS, unroll=2)
        def _(g):
            row = pl.multiple_of(start + g * ROWS, ROWS)
            at = pl.multiple_of(g * ROWS, ROWS)
            write_segment(
                load_blocks(own, row, 8, 16) + load_blocks(rim_next, row, 0, 8),
                jitter_1, taper, seg, at,
            )
            write_segment(
                load_blocks(rim_prev, row, 0, 8) + load_blocks(own, row, 0, 16),
                jitter_2, taper, seg, pl.multiple_of(size + g * ROWS, ROWS),
            )

        transform(2 * size)

        @pl.loop(0, size // ROWS, unroll=2)
        def _(g):
            row = pl.multiple_of(start + g * ROWS, ROWS)
            re, im = whiten_rows(spec, pl.multiple_of(g * ROWS, ROWS))
            white[1, pl.ds(row, ROWS), :NF] = re
            white[1, pl.ds(row, ROWS), NF:] = im
            re, im = whiten_rows(spec, pl.multiple_of(size + g * ROWS, ROWS))
            white[2, pl.ds(row, ROWS), :NF] = (re * keep).astype(jnp.bfloat16)
            white[2, pl.ds(row, ROWS), NF:] = (im * keep).astype(jnp.bfloat16)

    def finish_early_windows():
        end_swap(0, 0, 1)
        add_cross((0,), 0, stations, fresh=True)

        @pl.when(is_last)
        def _():
            end_swap(2, 3, 1)
            add_cross((3,), 0, stations)

    two_windows(0, 0, chunk)
    finish_early_windows()
    two_windows(1, chunk, chunk)
    if early:
        start_swap(1, 1, 2)

    @pl.loop(2, CHUNKS - 1)
    def _(c):
        two_windows(c, c * chunk, chunk)

    last = stations - chunk
    if early:
        end_swap(1, 1, 2)
        add_cross((1, 2), 0, last)
    two_windows(CHUNKS - 1, last, half)
    two_windows(CHUNKS, last + half, half)
    if not early:
        start_swap(1, 1, 2)
        end_swap(1, 1, 2)
    load_lags.wait()
    pending = last if early else 0

    span = pairs // PIECES

    def share(c, piece):
        return lax.dot_general(
            lags[pl.ds(pl.multiple_of(c * lag_rows, lag_rows), lag_rows)],
            cross[pl.ds(pl.multiple_of(piece * span, span), span)],
            (((1,), (1,)), ((), ())),
            preferred_element_type=jnp.float32,
        )

    def up(index):
        return pltpu.make_async_remote_copy(
            src_ref=up_send.at[index],
            dst_ref=up_recv.at[index],
            send_sem=up_send_sem.at[index],
            recv_sem=up_recv_sem.at[index],
            device_id={"tm": tm + 1},
            device_id_type=MESH,
        )

    def down(index):
        return pltpu.make_async_remote_copy(
            src_ref=down_send.at[index],
            dst_ref=down_recv.at[index],
            send_sem=down_send_sem.at[index],
            recv_sem=down_recv_sem.at[index],
            device_id={"tm": tm - 1},
            device_id_type=MESH,
        )

    @pl.loop(0, (n_tm - 1) * PIECES)
    def _(t):
        @pl.when(t < PIECES)
        def _():
            cross_part(t, (1, 2), pending, stations, final=True)

        up_item = t - tm
        up_chunk = n_tm - 1 - up_item // PIECES
        up_piece = up_item % PIECES

        @pl.when((up_item >= 0) & (up_item < (n_tm - 1 - tm) * PIECES))
        def _():
            index = up_chunk * PIECES + up_piece
            own_share = share(up_chunk, up_piece)

            @pl.when(has_prev)
            def _():
                up(index).wait_recv()
                up_send[index] = (own_share + up_recv[index].astype(jnp.float32)).astype(
                    jnp.bfloat16
                )

            @pl.when(tm == 0)
            def _():
                up_send[index] = own_share.astype(jnp.bfloat16)

            up(index).start()

        down_item = t - (n_tm - 1 - tm)
        down_chunk = down_item // PIECES
        down_piece = down_item % PIECES

        @pl.when((down_item >= 0) & (down_item < tm * PIECES))
        def _():
            index = down_chunk * PIECES + down_piece
            own_share = share(down_chunk, down_piece)

            @pl.when(has_next)
            def _():
                down(index).wait_recv()
                down_send[index] = (own_share + down_recv[index].astype(jnp.float32)).astype(
                    jnp.bfloat16
                )

            @pl.when(is_last)
            def _():
                down_send[index] = own_share.astype(jnp.bfloat16)

            down(index).start()

    scaling = 1.0 / math.sqrt(NF * 3 * n_tm)
    for piece in range(PIECES):
        index = tm * PIECES + piece
        columns = slice(piece * span, (piece + 1) * span)
        out[:, columns] = share(tm, piece) * scaling

    for piece in range(PIECES):
        index = tm * PIECES + piece
        columns = slice(piece * span, (piece + 1) * span)

        @pl.when(has_prev)
        def _():
            up(index).wait_recv()
            out[:, columns] += up_recv[index].astype(jnp.float32) * scaling

        @pl.when(has_next)
        def _():
            down(index).wait_recv()
            out[:, columns] += down_recv[index].astype(jnp.float32) * scaling

    @pl.when(has_next)
    def _():
        offset_up.wait_send()

    for c in range(CHUNKS + 1):

        @pl.when(has_next)
        def _():
            rim_up(c).wait_send()

        @pl.when(has_prev)
        def _():
            rim_down(c).wait_send()

    @pl.loop(0, n_tm * PIECES)
    def _(index):
        @pl.when(index >= (tm + 1) * PIECES)
        def _():
            up(index).wait_send()

        @pl.when(index < tm * PIECES)
        def _():
            down(index).wait_send()


def on_device(n_tm, n_sta, traces, offsets, pair_first, pair_slot, send_rows):
    stations = traces.shape[0]
    pairs = pair_first.shape[0]
    slots = n_sta * CAP
    lag_rows = NL // n_tm
    chunk = stations // CHUNKS
    items = n_tm * PIECES
    bf16, f32 = jnp.bfloat16, jnp.float32
    vmem = pl.BlockSpec(memory_space=pltpu.VMEM)
    smem = pl.BlockSpec(memory_space=pltpu.SMEM)
    hbm = pl.BlockSpec(memory_space=pl.ANY)
    dma = pltpu.SemaphoreType.DMA
    strip = pltpu.VMEM((items, lag_rows, pairs // PIECES), bf16)
    return pl.pallas_call(
        functools.partial(kernel, n_tm, n_sta),
        out_shape=jax.ShapeDtypeStruct((lag_rows, pairs), f32),
        in_specs=[smem, vmem, vmem, vmem, vmem, vmem, hbm, hbm, hbm],
        out_specs=vmem,
        scratch_shapes=[
            pltpu.VMEM((stations, TB), bf16),
            pltpu.VMEM((stations, TB), bf16),
            pltpu.VMEM((stations, STEP), bf16),
            pltpu.VMEM((stations, STEP), bf16),
            pltpu.VMEM((WIN, 2 * NF), bf16),
            pltpu.VMEM((NL, 2 * NF), bf16),
            pltpu.VMEM((stations, WIN), bf16),
            pltpu.VMEM((stations, 2 * NF), f32),
            pltpu.VMEM((stations, BLK), f32),
            pltpu.VMEM((4, stations, 2 * NF), bf16),
            pltpu.VMEM((4, slots, 2 * NF), bf16),
            pltpu.VMEM((4, slots, 2 * NF), bf16),
            pltpu.VMEM((pairs, stations), bf16),
            pltpu.VMEM((pairs, slots), bf16),
            pltpu.VMEM((slots, stations), bf16),
            pltpu.VMEM((stations, stations), bf16),
            pltpu.VMEM((pairs, stations), bf16),
            pltpu.VMEM((slots, stations), bf16),
            pltpu.VMEM((4, pairs, 2 * NF), bf16),
            pltpu.VMEM((pairs, 2 * NF), f32),
            pltpu.VMEM((pairs, 2 * NF), bf16),
            strip,
            strip,
            strip,
            strip,
            pltpu.VMEM((8, BLK), jnp.int32),
            pltpu.VMEM((8, BLK), jnp.int32),
            dma((5,)),
            dma((2, CHUNKS + 1)),
            dma((2, CHUNKS + 1)),
            dma((2,)),
            dma((3, n_sta)),
            dma((3, n_sta)),
            dma((items,)),
            dma((items,)),
            dma((items,)),
            dma((items,)),
        ],
        compiler_params=pltpu.CompilerParams(
            collective_id=0, has_side_effects=True, vmem_limit_bytes=56 * 1024 * 1024
        ),
    )(
        offsets,
        pair_first.reshape(1, pairs),
        pair_slot.reshape(1, pairs),
        send_rows,
        jnp.asarray(taper_table()),
        jnp.asarray(taper_rest()),
        traces,
        jnp.asarray(dft_table()),
        jnp.asarray(lag_table()),
    )


def solution(mesh):
    in_specs = (P("sta", ("day", "tm")), P(("day", "tm")), P("sta"), P("sta"), P("sta", None))
    out_specs = P(("day", "tm"), "sta")
    return jax.shard_map(
        functools.partial(on_device, mesh.shape["tm"], mesh.shape["sta"]),
        mesh=mesh,
        in_specs=in_specs,
        out_specs=out_specs,
        check_vma=False,
    )
```

```python
import functools
import math

import jax
import jax.numpy as jnp
import numpy as np
from jax import lax
from jax.experimental import pallas as pl
from jax.experimental.pallas import tpu as pltpu
from jax.sharding import PartitionSpec as P

WIN = 2048
NF = 512
NL = 1024
STEP = 1024
TB = 3072
CAP = 32
FAR_ROWS = 16
FLOOR = 0.1
CHUNKS = 4
PIECES = 2
BLK = 128
ROWS = 16
MESH = pl.DeviceIdType.MESH


def taper_table():
    n = np.arange(WIN, dtype=np.float64)
    return (0.5 - 0.5 * np.cos(2.0 * np.pi * n / WIN)).astype(np.float32)[None, :]


def dft_table():
    n = np.arange(WIN)[:, None]
    k = np.arange(NF)[None, :] + 1
    angle = (n * k % WIN) * (2.0 * np.pi / WIN)
    return np.concatenate([np.cos(angle), -np.sin(angle)], axis=1).astype(jnp.bfloat16)


def lag_table():
    t = np.arange(NL)[:, None] - NL // 2
    k = np.arange(NF)[None, :] + 1
    angle = (t * k % WIN) * (2.0 * np.pi / WIN)
    return np.concatenate([np.cos(angle), -np.sin(angle)], axis=1).astype(jnp.bfloat16)


def shifted(blocks, jitter):
    wanted = len(blocks) - 8
    quotient = jitter // BLK
    rest = jitter % BLK
    for bit, count in ((8, wanted + 8), (4, wanted + 4), (2, wanted + 2), (1, wanted + 1)):
        on = (quotient // bit) % 2 == 1
        blocks = [
            jnp.where(on, blocks[i + bit], blocks[i]) if i + bit < len(blocks) else blocks[i]
            for i in range(count)
        ]
    turn = (BLK - rest) % BLK
    rolled = [pltpu.roll(b, turn, 1) for b in blocks]
    lane = lax.broadcasted_iota(jnp.int32, blocks[0].shape, 1)
    keep = lane < BLK - rest
    return [jnp.where(keep, rolled[i], rolled[i + 1]) for i in range(wanted)]


def write_segment(blocks, jitter, taper, seg, row, means=None):
    values = [v.astype(jnp.float32) for v in shifted(blocks, jitter)]
    sums = values
    while len(sums) > 1:
        sums = [a + b for a, b in zip(sums[::2], sums[1::2])]
    total = sums[0]
    mean = jnp.sum(total, axis=1, keepdims=True) * (1.0 / WIN)
    if means is not None:
        means[pl.ds(row, ROWS)] = jnp.broadcast_to(mean, (ROWS, BLK))
    for i, v in enumerate(values):
        columns = slice(i * BLK, (i + 1) * BLK)
        seg[pl.ds(row, ROWS), columns] = ((v - mean) * taper[:, columns]).astype(jnp.bfloat16)


def taper_rest():
    rest = taper_table()[0, STEP:].astype(np.float64) @ dft_table()[STEP:].astype(np.float64)
    return rest.astype(np.float32)[None, :]


def load_blocks(ref, row, first, count):
    return [
        ref[pl.ds(row, ROWS), i * BLK : (i + 1) * BLK]
        for i in range(first, first + count)
    ]


def whiten_rows(spec, row):
    re = spec[pl.ds(row, ROWS), :NF]
    im = spec[pl.ds(row, ROWS), NF:]
    amplitude = jnp.sqrt(re * re + im * im + 1e-06)
    wide = jnp.concatenate([amplitude, jnp.zeros((ROWS, BLK), jnp.float32)], axis=1)
    width = NF + BLK
    pair = wide + pltpu.roll(wide, 1, 1)
    five = wide + pltpu.roll(pair, 1, 1) + pltpu.roll(pair, width - 2, 1)
    inverse = 1.0 / jnp.maximum(five[:, :NF] * (1.0 / 5.0), FLOOR)
    return (re * inverse).astype(jnp.bfloat16), (im * inverse).astype(jnp.bfloat16)


def kernel(
    n_tm, n_sta,
    offsets, pair_first, pair_slot, send_rows, taper, rest, traces, table_hbm, lag_hbm,
    out,
    raw, own, rim_prev, rim_next, table, lags, seg, spec, means, white, outgoing, incoming,
    pick_first, pick_second, pick_send, order, first_at, send_at, second_rows, cross_sum, cross,
    up_send, up_recv, down_send, down_recv, offset_send, offset_recv,
    local_sem, rim_send_sem, rim_recv_sem, offset_sem, swap_send_sem, swap_recv_sem,
    up_send_sem, up_recv_sem, down_send_sem, down_recv_sem,
):
    stations = own.shape[0]
    pairs = out.shape[1]
    lag_rows = out.shape[0]
    slots = n_sta * CAP
    chunk = stations // CHUNKS
    early = slots <= chunk
    tm = lax.axis_index("tm")
    me = lax.axis_index("sta")
    has_prev = tm > 0
    has_next = tm < n_tm - 1
    is_last = tm == n_tm - 1

    def load_columns(first, last, index):
        columns = pl.ds(first, last - first)
        return pltpu.make_async_copy(
            traces.at[:, columns], raw.at[:, columns], local_sem.at[index]
        )

    load_head = load_columns(0, STEP, 0)
    load_tail = load_columns(TB - STEP, TB, 1)
    load_middle = load_columns(STEP, TB - STEP, 2)
    load_table = pltpu.make_async_copy(table_hbm, table, local_sem.at[3])
    load_lags = pltpu.make_async_copy(lag_hbm, lags, local_sem.at[4])
    load_head.start()
    load_tail.start()

    incoming[...] = jnp.zeros_like(incoming)
    offset_send[...] = jnp.full(offset_send.shape, offsets[2], jnp.int32)

    @pl.when(tm == 0)
    def _():
        rim_prev[...] = jnp.zeros_like(rim_prev)
        offset_recv[...] = jnp.full(offset_recv.shape, 2 * STEP, jnp.int32)

    @pl.when(is_last)
    def _():
        rim_next[...] = jnp.zeros_like(rim_next)

    barrier = pltpu.get_barrier_semaphore()
    for delta in range(1, n_sta):
        pl.semaphore_signal(
            barrier, inc=1, device_id={"sta": (me + delta) % n_sta}, device_id_type=MESH
        )

    @pl.when(has_prev)
    def _():
        pl.semaphore_signal(barrier, inc=1, device_id={"tm": tm - 1}, device_id_type=MESH)

    @pl.when(has_next)
    def _():
        pl.semaphore_signal(barrier, inc=1, device_id={"tm": tm + 1}, device_id_type=MESH)

    def rim_rows(c):
        return pl.ds(c * chunk, chunk)

    def rim_up(c):
        rows = rim_rows(c)
        return pltpu.make_async_remote_copy(
            src_ref=own.at[rows, pl.ds(TB - STEP, STEP)],
            dst_ref=rim_prev.at[rows],
            send_sem=rim_send_sem.at[0, c],
            recv_sem=rim_recv_sem.at[0, c],
            device_id={"tm": tm + 1},
            device_id_type=MESH,
        )

    def rim_down(c):
        rows = rim_rows(c)
        return pltpu.make_async_remote_copy(
            src_ref=own.at[rows, pl.ds(0, STEP)],
            dst_ref=rim_next.at[rows],
            send_sem=rim_send_sem.at[1, c],
            recv_sem=rim_recv_sem.at[1, c],
            device_id={"tm": tm - 1},
            device_id_type=MESH,
        )

    offset_up = pltpu.make_async_remote_copy(
        src_ref=offset_send,
        dst_ref=offset_recv,
        send_sem=offset_sem.at[0],
        recv_sem=offset_sem.at[1],
        device_id={"tm": tm + 1},
        device_id_type=MESH,
    )

    def one_hot(ref, values, depth):
        count = values.shape[1]
        spread = jnp.transpose(jnp.broadcast_to(values.astype(jnp.float32), (BLK, count)))
        lane = lax.broadcasted_iota(jnp.int32, (count, BLK), 1).astype(jnp.float32)
        for b in range(depth // BLK):
            ref[:, b * BLK : (b + 1) * BLK] = (
                (spread == lane + float(b * BLK)).astype(jnp.float32).astype(jnp.bfloat16)
            )

    one_hot(pick_send, send_rows[...], stations)
    hits = jnp.dot(
        jnp.ones((8, slots), jnp.bfloat16), pick_send[...], preferred_element_type=jnp.float32
    )
    chosen = hits > 0.5
    mark = chosen.astype(jnp.float32)
    from_row = lax.broadcasted_iota(jnp.int32, (stations, stations), 0)
    to_lane = lax.broadcasted_iota(jnp.int32, (stations, stations), 1)
    up_to = (from_row <= to_lane).astype(jnp.float32).astype(jnp.bfloat16)
    running = jnp.dot(mark.astype(jnp.bfloat16), up_to, preferred_element_type=jnp.float32)
    lane = lax.broadcasted_iota(jnp.int32, (8, stations), 1).astype(jnp.float32)
    total = jnp.sum(mark, axis=1, keepdims=True)
    place = jnp.where(chosen, running - 1.0, total + lane - running)
    order[...] = (
        (place[:1] == from_row.astype(jnp.float32)).astype(jnp.float32).astype(jnp.bfloat16)
    )

    load_head.wait()
    load_tail.wait()
    load_middle.start()
    load_table.start()
    load_lags.start()

    def arrange(rows, columns):
        own[rows, columns] = jnp.dot(
            order[rows], raw[:, columns], preferred_element_type=jnp.float32
        ).astype(jnp.bfloat16)

    for c in range(CHUNKS):
        arrange(rim_rows(c), slice(0, STEP))
        arrange(rim_rows(c), slice(TB - STEP, TB))

        if c == 0:
            greeted = n_sta - 1 + has_prev.astype(jnp.int32) + has_next.astype(jnp.int32)
            pl.semaphore_wait(barrier, greeted)

            @pl.when(has_next)
            def _():
                offset_up.start()

        @pl.when(has_next)
        def _():
            rim_up(c).start()

        @pl.when(has_prev)
        def _():
            rim_down(c).start()

    load_middle.wait()
    arrange(slice(0, stations), slice(STEP, TB - STEP))

    def in_order(ref):
        return lax.dot_general(
            ref[...], order[...], (((1,), (1,)), ((), ())),
            preferred_element_type=jnp.float32,
        ).astype(jnp.bfloat16)

    one_hot(pick_first, pair_first[...], stations)
    one_hot(pick_second, pair_slot[...], slots)
    first_at[...] = in_order(pick_first)
    send_at[...] = in_order(pick_send)
    load_table.wait()

    scale = 1.0 / math.sqrt(WIN)

    def transform(count):
        spec[:count] = (
            jnp.dot(seg[:count], table[...], preferred_element_type=jnp.float32) * scale
        )

    def transform_half():
        first = jnp.dot(
            seg[:, :STEP], table[:STEP], preferred_element_type=jnp.float32
        )
        spec[...] = (first - means[:, :1] * rest[...]) * scale

    def whiten_group(slot, row):
        re, im = whiten_rows(spec, row)
        white[slot, pl.ds(row, ROWS), :NF] = re
        white[slot, pl.ds(row, ROWS), NF:] = im

    def whole_window(slot, jitter, blocks_at):
        batch = stations // 2

        @pl.loop(0, batch // ROWS, unroll=4)
        def _(g):
            row = pl.multiple_of(g * ROWS, ROWS)
            write_segment(blocks_at(row), jitter, taper, seg, row)

        width = 2 * NF // 4
        share = batch // ROWS // 4
        for b in range(2):
            rows = slice(b * batch, (b + 1) * batch)
            for j in range(4):
                columns = slice(j * width, (j + 1) * width)
                spec[rows, columns] = (
                    jnp.dot(seg[rows], table[:, columns], preferred_element_type=jnp.float32)
                    * scale
                )
                for g in range(j * share, (j + 1) * share):
                    if b == 0:
                        row = batch + g * ROWS
                        write_segment(blocks_at(row), jitter, taper, seg, row)
                    else:
                        whiten_group(slot, g * ROWS)

        @pl.loop(0, batch // ROWS, unroll=4)
        def _(g):
            whiten_group(slot, pl.multiple_of(batch + g * ROWS, ROWS))

    def half_window(slot, jitter, blocks_at):
        @pl.loop(0, stations // ROWS, unroll=4)
        def _(g):
            row = pl.multiple_of(g * ROWS, ROWS)
            write_segment(blocks_at(row), jitter, taper, seg, row, means)

        transform_half()

        @pl.loop(0, stations // ROWS, unroll=4)
        def _(g):
            whiten_group(slot, pl.multiple_of(g * ROWS, ROWS))

    def swap(which, slot, depth):
        result = []
        for delta in range(1, n_sta):
            rows = CAP if min(delta, n_sta - delta) <= 1 else FAR_ROWS
            partner = (me + delta) % n_sta
            result.append(
                pltpu.make_async_remote_copy(
                    src_ref=outgoing.at[
                        pl.ds(slot, depth), pl.ds(pl.multiple_of(partner * CAP, CAP), rows)
                    ],
                    dst_ref=incoming.at[
                        pl.ds(slot, depth), pl.ds(pl.multiple_of(me * CAP, CAP), rows)
                    ],
                    send_sem=swap_send_sem.at[which, delta],
                    recv_sem=swap_recv_sem.at[which, delta],
                    device_id={"sta": partner},
                    device_id_type=MESH,
                )
            )
        return result

    lead = min(slots, stations)

    def start_swap(which, slot, depth):
        for w in range(slot, slot + depth):
            outgoing[w] = jnp.dot(
                send_at[:, :lead], white[w, :lead], preferred_element_type=jnp.float32
            ).astype(jnp.bfloat16)
        for copy in swap(which, slot, depth):
            copy.start()
        mine = pl.ds(pl.multiple_of(me * CAP, CAP), CAP)
        for w in range(slot, slot + depth):
            incoming[w, mine] = outgoing[w, mine]

    def end_swap(which, slot, depth):
        for copy in swap(which, slot, depth):
            copy.wait()
        for w in range(slot, slot + depth):
            second_rows[w] = jnp.dot(
                pick_second[...], incoming[w], preferred_element_type=jnp.float32
            ).astype(jnp.bfloat16)

    part = pairs // PIECES
    width = 256

    def cross_part(p, windows, low, high, fresh=False, final=False):
        rows = pl.ds(pl.multiple_of(p * part, part), part)
        for b in range(NF // width):
            rcol = slice(b * width, (b + 1) * width)
            icol = slice(NF + b * width, NF + (b + 1) * width)
            real = None if fresh else cross_sum[rows, rcol]
            imag = None if fresh else cross_sum[rows, icol]
            for w in windows:
                fr, fi = [
                    jnp.dot(
                        first_at[rows, low:high], white[w, low:high, columns],
                        preferred_element_type=jnp.float32,
                    )
                    for columns in (rcol, icol)
                ]
                sr = second_rows[w, rows, rcol].astype(jnp.float32)
                si = second_rows[w, rows, icol].astype(jnp.float32)
                new_real = fr * sr + fi * si
                new_imag = fi * sr - fr * si
                real = new_real if real is None else real + new_real
                imag = new_imag if imag is None else imag + new_imag
            if final:
                cross[rows, rcol] = real.astype(jnp.bfloat16)
                cross[rows, icol] = imag.astype(jnp.bfloat16)
            else:
                cross_sum[rows, rcol] = real
                cross_sum[rows, icol] = imag

    def add_cross(windows, low, high, fresh=False):
        @pl.loop(0, PIECES)
        def _(p):
            cross_part(p, windows, low, high, fresh=fresh)

    whole_window(0, offsets[0], lambda row: load_blocks(own, row, 0, 24))
    start_swap(0, 0, 1)

    @pl.when(is_last)
    def _():
        half_window(
            3,
            offsets[2] - 2 * STEP,
            lambda row: load_blocks(own, row, 16, 8)
            + [jnp.zeros((ROWS, BLK), jnp.bfloat16)] * 8,
        )
        start_swap(2, 3, 1)

    @pl.when(has_prev)
    def _():
        offset_up.wait_recv()

    jitter_1 = offsets[1] - STEP
    jitter_2 = offset_recv[0, 0] - 2 * STEP
    keep = jnp.where(has_prev, 1.0, 0.0).astype(jnp.float32)

    def two_windows(c, start, size):
        @pl.when(has_prev)
        def _():
            rim_up(c).wait_recv()

        @pl.when(has_next)
        def _():
            rim_down(c).wait_recv()

        @pl.loop(0, size // ROWS, unroll=2)
        def _(g):
            row = pl.multiple_of(start + g * ROWS, ROWS)
            at = pl.multiple_of(g * ROWS, ROWS)
            write_segment(
                load_blocks(own, row, 8, 16) + load_blocks(rim_next, row, 0, 8),
                jitter_1, taper, seg, at,
            )
            write_segment(
                load_blocks(rim_prev, row, 0, 8) + load_blocks(own, row, 0, 16),
                jitter_2, taper, seg, pl.multiple_of(size + g * ROWS, ROWS),
            )

        transform(2 * size)

        @pl.loop(0, size // ROWS, unroll=2)
        def _(g):
            row = pl.multiple_of(start + g * ROWS, ROWS)
            re, im = whiten_rows(spec, pl.multiple_of(g * ROWS, ROWS))
            white[1, pl.ds(row, ROWS), :NF] = re
            white[1, pl.ds(row, ROWS), NF:] = im
            re, im = whiten_rows(spec, pl.multiple_of(size + g * ROWS, ROWS))
            white[2, pl.ds(row, ROWS), :NF] = (re * keep).astype(jnp.bfloat16)
            white[2, pl.ds(row, ROWS), NF:] = (im * keep).astype(jnp.bfloat16)

    def finish_early_windows():
        end_swap(0, 0, 1)
        add_cross((0,), 0, stations, fresh=True)

        @pl.when(is_last)
        def _():
            end_swap(2, 3, 1)
            add_cross((3,), 0, stations)

    two_windows(0, 0, chunk)
    if early:
        start_swap(1, 1, 2)
    finish_early_windows()

    @pl.loop(1, CHUNKS - 1)
    def _(c):
        two_windows(c, c * chunk, chunk)

    last = stations - chunk
    if early:
        end_swap(1, 1, 2)
        add_cross((1, 2), 0, last)
    two_windows(CHUNKS - 1, last, chunk)
    if not early:
        start_swap(1, 1, 2)
        end_swap(1, 1, 2)
    load_lags.wait()
    pending = last if early else 0

    span = pairs // PIECES

    def share(c, piece):
        return lax.dot_general(
            lags[pl.ds(pl.multiple_of(c * lag_rows, lag_rows), lag_rows)],
            cross[pl.ds(pl.multiple_of(piece * span, span), span)],
            (((1,), (1,)), ((), ())),
            preferred_element_type=jnp.float32,
        )

    def up(index):
        return pltpu.make_async_remote_copy(
            src_ref=up_send.at[index],
            dst_ref=up_recv.at[index],
            send_sem=up_send_sem.at[index],
            recv_sem=up_recv_sem.at[index],
            device_id={"tm": tm + 1},
            device_id_type=MESH,
        )

    def down(index):
        return pltpu.make_async_remote_copy(
            src_ref=down_send.at[index],
            dst_ref=down_recv.at[index],
            send_sem=down_send_sem.at[index],
            recv_sem=down_recv_sem.at[index],
            device_id={"tm": tm - 1},
            device_id_type=MESH,
        )

    @pl.loop(0, (n_tm - 1) * PIECES)
    def _(t):
        @pl.when(t < PIECES)
        def _():
            cross_part(t, (1, 2), pending, stations, final=True)

        up_item = t - tm
        up_chunk = n_tm - 1 - up_item // PIECES
        up_piece = up_item % PIECES

        @pl.when((up_item >= 0) & (up_item < (n_tm - 1 - tm) * PIECES))
        def _():
            index = up_chunk * PIECES + up_piece
            own_share = share(up_chunk, up_piece)

            @pl.when(has_prev)
            def _():
                up(index).wait_recv()
                up_send[index] = (own_share + up_recv[index].astype(jnp.float32)).astype(
                    jnp.bfloat16
                )

            @pl.when(tm == 0)
            def _():
                up_send[index] = own_share.astype(jnp.bfloat16)

            up(index).start()

        down_item = t - (n_tm - 1 - tm)
        down_chunk = down_item // PIECES
        down_piece = down_item % PIECES

        @pl.when((down_item >= 0) & (down_item < tm * PIECES))
        def _():
            index = down_chunk * PIECES + down_piece
            own_share = share(down_chunk, down_piece)

            @pl.when(has_next)
            def _():
                down(index).wait_recv()
                down_send[index] = (own_share + down_recv[index].astype(jnp.float32)).astype(
                    jnp.bfloat16
                )

            @pl.when(is_last)
            def _():
                down_send[index] = own_share.astype(jnp.bfloat16)

            down(index).start()

    scaling = 1.0 / math.sqrt(NF * 3 * n_tm)
    for piece in range(PIECES):
        index = tm * PIECES + piece
        columns = slice(piece * span, (piece + 1) * span)
        out[:, columns] = share(tm, piece) * scaling

    for piece in range(PIECES):
        index = tm * PIECES + piece
        columns = slice(piece * span, (piece + 1) * span)

        @pl.when(has_prev)
        def _():
            up(index).wait_recv()
            out[:, columns] += up_recv[index].astype(jnp.float32) * scaling

        @pl.when(has_next)
        def _():
            down(index).wait_recv()
            out[:, columns] += down_recv[index].astype(jnp.float32) * scaling

    @pl.when(has_next)
    def _():
        offset_up.wait_send()

    for c in range(CHUNKS):

        @pl.when(has_next)
        def _():
            rim_up(c).wait_send()

        @pl.when(has_prev)
        def _():
            rim_down(c).wait_send()

    @pl.loop(0, n_tm * PIECES)
    def _(index):
        @pl.when(index >= (tm + 1) * PIECES)
        def _():
            up(index).wait_send()

        @pl.when(index < tm * PIECES)
        def _():
            down(index).wait_send()


def on_device(n_tm, n_sta, traces, offsets, pair_first, pair_slot, send_rows):
    stations = traces.shape[0]
    pairs = pair_first.shape[0]
    slots = n_sta * CAP
    lag_rows = NL // n_tm
    chunk = stations // CHUNKS
    items = n_tm * PIECES
    bf16, f32 = jnp.bfloat16, jnp.float32
    vmem = pl.BlockSpec(memory_space=pltpu.VMEM)
    smem = pl.BlockSpec(memory_space=pltpu.SMEM)
    hbm = pl.BlockSpec(memory_space=pl.ANY)
    dma = pltpu.SemaphoreType.DMA
    strip = pltpu.VMEM((items, lag_rows, pairs // PIECES), bf16)
    return pl.pallas_call(
        functools.partial(kernel, n_tm, n_sta),
        out_shape=jax.ShapeDtypeStruct((lag_rows, pairs), f32),
        in_specs=[smem, vmem, vmem, vmem, vmem, vmem, hbm, hbm, hbm],
        out_specs=vmem,
        scratch_shapes=[
            pltpu.VMEM((stations, TB), bf16),
            pltpu.VMEM((stations, TB), bf16),
            pltpu.VMEM((stations, STEP), bf16),
            pltpu.VMEM((stations, STEP), bf16),
            pltpu.VMEM((WIN, 2 * NF), bf16),
            pltpu.VMEM((NL, 2 * NF), bf16),
            pltpu.VMEM((stations, WIN), bf16),
            pltpu.VMEM((stations, 2 * NF), f32),
            pltpu.VMEM((stations, BLK), f32),
            pltpu.VMEM((4, stations, 2 * NF), bf16),
            pltpu.VMEM((4, slots, 2 * NF), bf16),
            pltpu.VMEM((4, slots, 2 * NF), bf16),
            pltpu.VMEM((pairs, stations), bf16),
            pltpu.VMEM((pairs, slots), bf16),
            pltpu.VMEM((slots, stations), bf16),
            pltpu.VMEM((stations, stations), bf16),
            pltpu.VMEM((pairs, stations), bf16),
            pltpu.VMEM((slots, stations), bf16),
            pltpu.VMEM((4, pairs, 2 * NF), bf16),
            pltpu.VMEM((pairs, 2 * NF), f32),
            pltpu.VMEM((pairs, 2 * NF), bf16),
            strip,
            strip,
            strip,
            strip,
            pltpu.VMEM((8, BLK), jnp.int32),
            pltpu.VMEM((8, BLK), jnp.int32),
            dma((5,)),
            dma((2, CHUNKS)),
            dma((2, CHUNKS)),
            dma((2,)),
            dma((3, n_sta)),
            dma((3, n_sta)),
            dma((items,)),
            dma((items,)),
            dma((items,)),
            dma((items,)),
        ],
        compiler_params=pltpu.CompilerParams(
            collective_id=0, has_side_effects=True, vmem_limit_bytes=56 * 1024 * 1024
        ),
    )(
        offsets,
        pair_first.reshape(1, pairs),
        pair_slot.reshape(1, pairs),
        send_rows,
        jnp.asarray(taper_table()),
        jnp.asarray(taper_rest()),
        traces,
        jnp.asarray(dft_table()),
        jnp.asarray(lag_table()),
    )


def solution(mesh):
    in_specs = (P("sta", ("day", "tm")), P(("day", "tm")), P("sta"), P("sta"), P("sta", None))
    out_specs = P(("day", "tm"), "sta")
    return jax.shard_map(
        functools.partial(on_device, mesh.shape["tm"], mesh.shape["sta"]),
        mesh=mesh,
        in_specs=in_specs,
        out_specs=out_specs,
        check_vma=False,
    )
```

```python
import functools
import math

import jax
import jax.numpy as jnp
import numpy as np
from jax import lax
from jax.experimental import pallas as pl
from jax.experimental.pallas import tpu as pltpu
from jax.sharding import PartitionSpec as P

WIN = 2048
NF = 512
NL = 1024
STEP = 1024
TB = 3072
CAP = 32
FAR_ROWS = 16
FLOOR = 0.1
CHUNKS = 4
PIECES = 2
BLK = 128
ROWS = 16
MESH = pl.DeviceIdType.MESH


def taper_table():
    n = np.arange(WIN, dtype=np.float64)
    return (0.5 - 0.5 * np.cos(2.0 * np.pi * n / WIN)).astype(np.float32)[None, :]


def dft_table():
    n = np.arange(WIN)[:, None]
    k = np.arange(NF)[None, :] + 1
    angle = (n * k % WIN) * (2.0 * np.pi / WIN)
    return np.concatenate([np.cos(angle), -np.sin(angle)], axis=1).astype(jnp.bfloat16)


def lag_table():
    t = np.arange(NL)[:, None] - NL // 2
    k = np.arange(NF)[None, :] + 1
    angle = (t * k % WIN) * (2.0 * np.pi / WIN)
    return np.concatenate([np.cos(angle), -np.sin(angle)], axis=1).astype(jnp.bfloat16)


def shifted(blocks, jitter):
    wanted = len(blocks) - 8
    quotient = jitter // BLK
    rest = jitter % BLK
    for bit, count in ((8, wanted + 8), (4, wanted + 4), (2, wanted + 2), (1, wanted + 1)):
        on = (quotient // bit) % 2 == 1
        blocks = [
            jnp.where(on, blocks[i + bit], blocks[i]) if i + bit < len(blocks) else blocks[i]
            for i in range(count)
        ]
    turn = (BLK - rest) % BLK
    rolled = [pltpu.roll(b, turn, 1) for b in blocks]
    lane = lax.broadcasted_iota(jnp.int32, blocks[0].shape, 1)
    keep = lane < BLK - rest
    return [jnp.where(keep, rolled[i], rolled[i + 1]) for i in range(wanted)]


def write_segment(blocks, jitter, taper, seg, row, means=None):
    values = [v.astype(jnp.float32) for v in shifted(blocks, jitter)]
    sums = values
    while len(sums) > 1:
        sums = [a + b for a, b in zip(sums[::2], sums[1::2])]
    total = sums[0]
    mean = jnp.sum(total, axis=1, keepdims=True) * (1.0 / WIN)
    if means is not None:
        means[pl.ds(row, ROWS)] = jnp.broadcast_to(mean, (ROWS, BLK))
    for i, v in enumerate(values):
        columns = slice(i * BLK, (i + 1) * BLK)
        seg[pl.ds(row, ROWS), columns] = ((v - mean) * taper[:, columns]).astype(jnp.bfloat16)


def taper_rest():
    rest = taper_table()[0, STEP:].astype(np.float64) @ dft_table()[STEP:].astype(np.float64)
    return rest.astype(np.float32)[None, :]


def load_blocks(ref, row, first, count):
    return [
        ref[pl.ds(row, ROWS), i * BLK : (i + 1) * BLK]
        for i in range(first, first + count)
    ]


def whiten_rows(spec, row):
    re = spec[pl.ds(row, ROWS), :NF]
    im = spec[pl.ds(row, ROWS), NF:]
    amplitude = jnp.sqrt(re * re + im * im + 1e-06)
    wide = jnp.concatenate([amplitude, jnp.zeros((ROWS, BLK), jnp.float32)], axis=1)
    width = NF + BLK
    pair = wide + pltpu.roll(wide, 1, 1)
    five = wide + pltpu.roll(pair, 1, 1) + pltpu.roll(pair, width - 2, 1)
    inverse = 1.0 / jnp.maximum(five[:, :NF] * (1.0 / 5.0), FLOOR)
    return (re * inverse).astype(jnp.bfloat16), (im * inverse).astype(jnp.bfloat16)


def kernel(
    n_tm, n_sta,
    offsets, pair_first, pair_slot, send_rows, taper, rest, traces, table_hbm, lag_hbm,
    out,
    raw, own, rim_prev, rim_next, table, lags, seg, spec, means, white, outgoing, incoming,
    pick_first, pick_second, pick_send, order, first_at, send_at, second_rows, cross_sum, cross,
    up_send, up_recv, down_send, down_recv, offset_send, offset_recv,
    local_sem, rim_send_sem, rim_recv_sem, offset_sem, swap_send_sem, swap_recv_sem,
    up_send_sem, up_recv_sem, down_send_sem, down_recv_sem,
):
    stations = own.shape[0]
    pairs = out.shape[1]
    lag_rows = out.shape[0]
    slots = n_sta * CAP
    chunk = stations // CHUNKS
    early = slots <= chunk
    tm = lax.axis_index("tm")
    me = lax.axis_index("sta")
    has_prev = tm > 0
    has_next = tm < n_tm - 1
    is_last = tm == n_tm - 1

    def load_columns(first, last, index):
        columns = pl.ds(first, last - first)
        return pltpu.make_async_copy(
            traces.at[:, columns], raw.at[:, columns], local_sem.at[index]
        )

    load_head = load_columns(0, STEP, 0)
    load_tail = load_columns(TB - STEP, TB, 1)
    load_middle = load_columns(STEP, TB - STEP, 2)
    load_table = pltpu.make_async_copy(table_hbm, table, local_sem.at[3])
    load_lags = pltpu.make_async_copy(lag_hbm, lags, local_sem.at[4])
    load_head.start()
    load_tail.start()

    incoming[...] = jnp.zeros_like(incoming)
    offset_send[...] = jnp.full(offset_send.shape, offsets[2], jnp.int32)

    @pl.when(tm == 0)
    def _():
        rim_prev[...] = jnp.zeros_like(rim_prev)
        offset_recv[...] = jnp.full(offset_recv.shape, 2 * STEP, jnp.int32)

    @pl.when(is_last)
    def _():
        rim_next[...] = jnp.zeros_like(rim_next)

    barrier = pltpu.get_barrier_semaphore()
    for delta in range(1, n_sta):
        pl.semaphore_signal(
            barrier, inc=1, device_id={"sta": (me + delta) % n_sta}, device_id_type=MESH
        )

    @pl.when(has_prev)
    def _():
        pl.semaphore_signal(barrier, inc=1, device_id={"tm": tm - 1}, device_id_type=MESH)

    @pl.when(has_next)
    def _():
        pl.semaphore_signal(barrier, inc=1, device_id={"tm": tm + 1}, device_id_type=MESH)

    def rim_rows(c):
        return pl.ds(c * chunk, chunk)

    def rim_up(c):
        rows = rim_rows(c)
        return pltpu.make_async_remote_copy(
            src_ref=own.at[rows, pl.ds(TB - STEP, STEP)],
            dst_ref=rim_prev.at[rows],
            send_sem=rim_send_sem.at[0, c],
            recv_sem=rim_recv_sem.at[0, c],
            device_id={"tm": tm + 1},
            device_id_type=MESH,
        )

    def rim_down(c):
        rows = rim_rows(c)
        return pltpu.make_async_remote_copy(
            src_ref=own.at[rows, pl.ds(0, STEP)],
            dst_ref=rim_next.at[rows],
            send_sem=rim_send_sem.at[1, c],
            recv_sem=rim_recv_sem.at[1, c],
            device_id={"tm": tm - 1},
            device_id_type=MESH,
        )

    offset_up = pltpu.make_async_remote_copy(
        src_ref=offset_send,
        dst_ref=offset_recv,
        send_sem=offset_sem.at[0],
        recv_sem=offset_sem.at[1],
        device_id={"tm": tm + 1},
        device_id_type=MESH,
    )

    def one_hot(ref, values, depth):
        count = values.shape[1]
        spread = jnp.transpose(jnp.broadcast_to(values.astype(jnp.float32), (BLK, count)))
        lane = lax.broadcasted_iota(jnp.int32, (count, BLK), 1).astype(jnp.float32)
        for b in range(depth // BLK):
            ref[:, b * BLK : (b + 1) * BLK] = (
                (spread == lane + float(b * BLK)).astype(jnp.float32).astype(jnp.bfloat16)
            )

    one_hot(pick_send, send_rows[...], stations)
    hits = jnp.dot(
        jnp.ones((8, slots), jnp.bfloat16), pick_send[...], preferred_element_type=jnp.float32
    )
    chosen = hits > 0.5
    mark = chosen.astype(jnp.float32)
    from_row = lax.broadcasted_iota(jnp.int32, (stations, stations), 0)
    to_lane = lax.broadcasted_iota(jnp.int32, (stations, stations), 1)
    up_to = (from_row <= to_lane).astype(jnp.float32).astype(jnp.bfloat16)
    running = jnp.dot(mark.astype(jnp.bfloat16), up_to, preferred_element_type=jnp.float32)
    lane = lax.broadcasted_iota(jnp.int32, (8, stations), 1).astype(jnp.float32)
    total = jnp.sum(mark, axis=1, keepdims=True)
    place = jnp.where(chosen, running - 1.0, total + lane - running)
    order[...] = (
        (place[:1] == from_row.astype(jnp.float32)).astype(jnp.float32).astype(jnp.bfloat16)
    )

    load_head.wait()
    load_tail.wait()
    load_middle.start()
    load_table.start()
    load_lags.start()

    def arrange(rows, columns):
        own[rows, columns] = jnp.dot(
            order[rows], raw[:, columns], preferred_element_type=jnp.float32
        ).astype(jnp.bfloat16)

    for c in range(CHUNKS):
        arrange(rim_rows(c), slice(0, STEP))
        arrange(rim_rows(c), slice(TB - STEP, TB))

        if c == 0:
            greeted = n_sta - 1 + has_prev.astype(jnp.int32) + has_next.astype(jnp.int32)
            pl.semaphore_wait(barrier, greeted)

            @pl.when(has_next)
            def _():
                offset_up.start()

        @pl.when(has_next)
        def _():
            rim_up(c).start()

        @pl.when(has_prev)
        def _():
            rim_down(c).start()

    load_middle.wait()
    arrange(slice(0, stations), slice(STEP, TB - STEP))

    def in_order(ref):
        return lax.dot_general(
            ref[...], order[...], (((1,), (1,)), ((), ())),
            preferred_element_type=jnp.float32,
        ).astype(jnp.bfloat16)

    one_hot(pick_first, pair_first[...], stations)
    one_hot(pick_second, pair_slot[...], slots)
    first_at[...] = in_order(pick_first)
    send_at[...] = in_order(pick_send)
    load_table.wait()

    scale = 1.0 / math.sqrt(WIN)

    def transform(count):
        spec[:count] = (
            jnp.dot(seg[:count], table[...], preferred_element_type=jnp.float32) * scale
        )

    def transform_half():
        first = jnp.dot(
            seg[:, :STEP], table[:STEP], preferred_element_type=jnp.float32
        )
        spec[...] = (first - means[:, :1] * rest[...]) * scale

    def whiten_group(slot, row):
        re, im = whiten_rows(spec, row)
        white[slot, pl.ds(row, ROWS), :NF] = re
        white[slot, pl.ds(row, ROWS), NF:] = im

    def whole_window(slot, jitter, blocks_at):
        batch = stations // 2

        @pl.loop(0, batch // ROWS, unroll=4)
        def _(g):
            row = pl.multiple_of(g * ROWS, ROWS)
            write_segment(blocks_at(row), jitter, taper, seg, row)

        width = 2 * NF // 4
        share = batch // ROWS // 4
        for b in range(2):
            rows = slice(b * batch, (b + 1) * batch)
            for j in range(4):
                columns = slice(j * width, (j + 1) * width)
                spec[rows, columns] = (
                    jnp.dot(seg[rows], table[:, columns], preferred_element_type=jnp.float32)
                    * scale
                )
                for g in range(j * share, (j + 1) * share):
                    if b == 0:
                        row = batch + g * ROWS
                        write_segment(blocks_at(row), jitter, taper, seg, row)
                    else:
                        whiten_group(slot, g * ROWS)

        @pl.loop(0, batch // ROWS, unroll=4)
        def _(g):
            whiten_group(slot, pl.multiple_of(batch + g * ROWS, ROWS))

    def half_window(slot, jitter, blocks_at):
        @pl.loop(0, stations // ROWS, unroll=4)
        def _(g):
            row = pl.multiple_of(g * ROWS, ROWS)
            write_segment(blocks_at(row), jitter, taper, seg, row, means)

        transform_half()

        @pl.loop(0, stations // ROWS, unroll=4)
        def _(g):
            whiten_group(slot, pl.multiple_of(g * ROWS, ROWS))

    def swap(which, slot, depth):
        result = []
        for delta in range(1, n_sta):
            rows = CAP if min(delta, n_sta - delta) <= 1 else FAR_ROWS
            partner = (me + delta) % n_sta
            result.append(
                pltpu.make_async_remote_copy(
                    src_ref=outgoing.at[
                        pl.ds(slot, depth), pl.ds(pl.multiple_of(partner * CAP, CAP), rows)
                    ],
                    dst_ref=incoming.at[
                        pl.ds(slot, depth), pl.ds(pl.multiple_of(me * CAP, CAP), rows)
                    ],
                    send_sem=swap_send_sem.at[which, delta],
                    recv_sem=swap_recv_sem.at[which, delta],
                    device_id={"sta": partner},
                    device_id_type=MESH,
                )
            )
        return result

    lead = min(slots, stations)

    def start_swap(which, slot, depth):
        for w in range(slot, slot + depth):
            outgoing[w] = jnp.dot(
                send_at[:, :lead], white[w, :lead], preferred_element_type=jnp.float32
            ).astype(jnp.bfloat16)
        for copy in swap(which, slot, depth):
            copy.start()
        mine = pl.ds(pl.multiple_of(me * CAP, CAP), CAP)
        for w in range(slot, slot + depth):
            incoming[w, mine] = outgoing[w, mine]

    def end_swap(which, slot, depth):
        for copy in swap(which, slot, depth):
            copy.wait()
        for w in range(slot, slot + depth):
            second_rows[w] = jnp.dot(
                pick_second[...], incoming[w], preferred_element_type=jnp.float32
            ).astype(jnp.bfloat16)

    part = pairs // PIECES
    width = 256

    def cross_part(p, windows, low, high, fresh=False, final=False):
        rows = pl.ds(pl.multiple_of(p * part, part), part)
        for b in range(NF // width):
            rcol = slice(b * width, (b + 1) * width)
            icol = slice(NF + b * width, NF + (b + 1) * width)
            real = None if fresh else cross_sum[rows, rcol]
            imag = None if fresh else cross_sum[rows, icol]
            for w in windows:
                fr, fi = [
                    jnp.dot(
                        first_at[rows, low:high], white[w, low:high, columns],
                        preferred_element_type=jnp.float32,
                    )
                    for columns in (rcol, icol)
                ]
                sr = second_rows[w, rows, rcol].astype(jnp.float32)
                si = second_rows[w, rows, icol].astype(jnp.float32)
                new_real = fr * sr + fi * si
                new_imag = fi * sr - fr * si
                real = new_real if real is None else real + new_real
                imag = new_imag if imag is None else imag + new_imag
            if final:
                cross[rows, rcol] = real.astype(jnp.bfloat16)
                cross[rows, icol] = imag.astype(jnp.bfloat16)
            else:
                cross_sum[rows, rcol] = real
                cross_sum[rows, icol] = imag

    def add_cross(windows, low, high, fresh=False):
        @pl.loop(0, PIECES)
        def _(p):
            cross_part(p, windows, low, high, fresh=fresh)

    whole_window(0, offsets[0], lambda row: load_blocks(own, row, 0, 24))
    start_swap(0, 0, 1)

    @pl.when(is_last)
    def _():
        half_window(
            3,
            offsets[2] - 2 * STEP,
            lambda row: load_blocks(own, row, 16, 8)
            + [jnp.zeros((ROWS, BLK), jnp.bfloat16)] * 8,
        )
        start_swap(2, 3, 1)

    @pl.when(has_prev)
    def _():
        offset_up.wait_recv()

    jitter_1 = offsets[1] - STEP
    jitter_2 = offset_recv[0, 0] - 2 * STEP
    keep = jnp.where(has_prev, 1.0, 0.0).astype(jnp.float32)

    def two_windows(c, start, size):
        @pl.when(has_prev)
        def _():
            rim_up(c).wait_recv()

        @pl.when(has_next)
        def _():
            rim_down(c).wait_recv()

        @pl.loop(0, size // ROWS, unroll=4)
        def _(g):
            row = pl.multiple_of(start + g * ROWS, ROWS)
            at = pl.multiple_of(g * ROWS, ROWS)
            write_segment(
                load_blocks(own, row, 8, 16) + load_blocks(rim_next, row, 0, 8),
                jitter_1, taper, seg, at,
            )
            write_segment(
                load_blocks(rim_prev, row, 0, 8) + load_blocks(own, row, 0, 16),
                jitter_2, taper, seg, pl.multiple_of(size + g * ROWS, ROWS),
            )

        transform(2 * size)

        @pl.loop(0, size // ROWS, unroll=4)
        def _(g):
            row = pl.multiple_of(start + g * ROWS, ROWS)
            re, im = whiten_rows(spec, pl.multiple_of(g * ROWS, ROWS))
            white[1, pl.ds(row, ROWS), :NF] = re
            white[1, pl.ds(row, ROWS), NF:] = im
            re, im = whiten_rows(spec, pl.multiple_of(size + g * ROWS, ROWS))
            white[2, pl.ds(row, ROWS), :NF] = (re * keep).astype(jnp.bfloat16)
            white[2, pl.ds(row, ROWS), NF:] = (im * keep).astype(jnp.bfloat16)

    def finish_early_windows():
        end_swap(0, 0, 1)
        add_cross((0,), 0, stations, fresh=True)

        @pl.when(is_last)
        def _():
            end_swap(2, 3, 1)
            add_cross((3,), 0, stations)

    two_windows(0, 0, chunk)
    if early:
        start_swap(1, 1, 2)
    finish_early_windows()

    @pl.loop(1, CHUNKS - 1)
    def _(c):
        two_windows(c, c * chunk, chunk)

    last = stations - chunk
    if early:
        end_swap(1, 1, 2)
        add_cross((1, 2), 0, last)
    two_windows(CHUNKS - 1, last, chunk)
    if not early:
        start_swap(1, 1, 2)
        end_swap(1, 1, 2)
    load_lags.wait()
    pending = last if early else 0

    span = pairs // PIECES

    def share(c, piece):
        return lax.dot_general(
            lags[pl.ds(pl.multiple_of(c * lag_rows, lag_rows), lag_rows)],
            cross[pl.ds(pl.multiple_of(piece * span, span), span)],
            (((1,), (1,)), ((), ())),
            preferred_element_type=jnp.float32,
        )

    def up(index):
        return pltpu.make_async_remote_copy(
            src_ref=up_send.at[index],
            dst_ref=up_recv.at[index],
            send_sem=up_send_sem.at[index],
            recv_sem=up_recv_sem.at[index],
            device_id={"tm": tm + 1},
            device_id_type=MESH,
        )

    def down(index):
        return pltpu.make_async_remote_copy(
            src_ref=down_send.at[index],
            dst_ref=down_recv.at[index],
            send_sem=down_send_sem.at[index],
            recv_sem=down_recv_sem.at[index],
            device_id={"tm": tm - 1},
            device_id_type=MESH,
        )

    @pl.loop(0, (n_tm - 1) * PIECES)
    def _(t):
        @pl.when(t < PIECES)
        def _():
            cross_part(t, (1, 2), pending, stations, final=True)

        up_item = t - tm
        up_chunk = n_tm - 1 - up_item // PIECES
        up_piece = up_item % PIECES

        @pl.when((up_item >= 0) & (up_item < (n_tm - 1 - tm) * PIECES))
        def _():
            index = up_chunk * PIECES + up_piece
            own_share = share(up_chunk, up_piece)

            @pl.when(has_prev)
            def _():
                up(index).wait_recv()
                up_send[index] = (own_share + up_recv[index].astype(jnp.float32)).astype(
                    jnp.bfloat16
                )

            @pl.when(tm == 0)
            def _():
                up_send[index] = own_share.astype(jnp.bfloat16)

            up(index).start()

        down_item = t - (n_tm - 1 - tm)
        down_chunk = down_item // PIECES
        down_piece = down_item % PIECES

        @pl.when((down_item >= 0) & (down_item < tm * PIECES))
        def _():
            index = down_chunk * PIECES + down_piece
            own_share = share(down_chunk, down_piece)

            @pl.when(has_next)
            def _():
                down(index).wait_recv()
                down_send[index] = (own_share + down_recv[index].astype(jnp.float32)).astype(
                    jnp.bfloat16
                )

            @pl.when(is_last)
            def _():
                down_send[index] = own_share.astype(jnp.bfloat16)

            down(index).start()

    scaling = 1.0 / math.sqrt(NF * 3 * n_tm)
    for piece in range(PIECES):
        index = tm * PIECES + piece
        columns = slice(piece * span, (piece + 1) * span)
        out[:, columns] = share(tm, piece) * scaling

    for piece in range(PIECES):
        index = tm * PIECES + piece
        columns = slice(piece * span, (piece + 1) * span)

        @pl.when(has_prev)
        def _():
            up(index).wait_recv()
            out[:, columns] += up_recv[index].astype(jnp.float32) * scaling

        @pl.when(has_next)
        def _():
            down(index).wait_recv()
            out[:, columns] += down_recv[index].astype(jnp.float32) * scaling

    @pl.when(has_next)
    def _():
        offset_up.wait_send()

    for c in range(CHUNKS):

        @pl.when(has_next)
        def _():
            rim_up(c).wait_send()

        @pl.when(has_prev)
        def _():
            rim_down(c).wait_send()

    @pl.loop(0, n_tm * PIECES)
    def _(index):
        @pl.when(index >= (tm + 1) * PIECES)
        def _():
            up(index).wait_send()

        @pl.when(index < tm * PIECES)
        def _():
            down(index).wait_send()


def on_device(n_tm, n_sta, traces, offsets, pair_first, pair_slot, send_rows):
    stations = traces.shape[0]
    pairs = pair_first.shape[0]
    slots = n_sta * CAP
    lag_rows = NL // n_tm
    chunk = stations // CHUNKS
    items = n_tm * PIECES
    bf16, f32 = jnp.bfloat16, jnp.float32
    vmem = pl.BlockSpec(memory_space=pltpu.VMEM)
    smem = pl.BlockSpec(memory_space=pltpu.SMEM)
    hbm = pl.BlockSpec(memory_space=pl.ANY)
    dma = pltpu.SemaphoreType.DMA
    strip = pltpu.VMEM((items, lag_rows, pairs // PIECES), bf16)
    return pl.pallas_call(
        functools.partial(kernel, n_tm, n_sta),
        out_shape=jax.ShapeDtypeStruct((lag_rows, pairs), f32),
        in_specs=[smem, vmem, vmem, vmem, vmem, vmem, hbm, hbm, hbm],
        out_specs=vmem,
        scratch_shapes=[
            pltpu.VMEM((stations, TB), bf16),
            pltpu.VMEM((stations, TB), bf16),
            pltpu.VMEM((stations, STEP), bf16),
            pltpu.VMEM((stations, STEP), bf16),
            pltpu.VMEM((WIN, 2 * NF), bf16),
            pltpu.VMEM((NL, 2 * NF), bf16),
            pltpu.VMEM((stations, WIN), bf16),
            pltpu.VMEM((stations, 2 * NF), f32),
            pltpu.VMEM((stations, BLK), f32),
            pltpu.VMEM((4, stations, 2 * NF), bf16),
            pltpu.VMEM((4, slots, 2 * NF), bf16),
            pltpu.VMEM((4, slots, 2 * NF), bf16),
            pltpu.VMEM((pairs, stations), bf16),
            pltpu.VMEM((pairs, slots), bf16),
            pltpu.VMEM((slots, stations), bf16),
            pltpu.VMEM((stations, stations), bf16),
            pltpu.VMEM((pairs, stations), bf16),
            pltpu.VMEM((slots, stations), bf16),
            pltpu.VMEM((4, pairs, 2 * NF), bf16),
            pltpu.VMEM((pairs, 2 * NF), f32),
            pltpu.VMEM((pairs, 2 * NF), bf16),
            strip,
            strip,
            strip,
            strip,
            pltpu.VMEM((8, BLK), jnp.int32),
            pltpu.VMEM((8, BLK), jnp.int32),
            dma((5,)),
            dma((2, CHUNKS)),
            dma((2, CHUNKS)),
            dma((2,)),
            dma((3, n_sta)),
            dma((3, n_sta)),
            dma((items,)),
            dma((items,)),
            dma((items,)),
            dma((items,)),
        ],
        compiler_params=pltpu.CompilerParams(
            collective_id=0, has_side_effects=True, vmem_limit_bytes=56 * 1024 * 1024
        ),
    )(
        offsets,
        pair_first.reshape(1, pairs),
        pair_slot.reshape(1, pairs),
        send_rows,
        jnp.asarray(taper_table()),
        jnp.asarray(taper_rest()),
        traces,
        jnp.asarray(dft_table()),
        jnp.asarray(lag_table()),
    )


def solution(mesh):
    in_specs = (P("sta", ("day", "tm")), P(("day", "tm")), P("sta"), P("sta"), P("sta", None))
    out_specs = P(("day", "tm"), "sta")
    return jax.shard_map(
        functools.partial(on_device, mesh.shape["tm"], mesh.shape["sta"]),
        mesh=mesh,
        in_specs=in_specs,
        out_specs=out_specs,
        check_vma=False,
    )
```
